512 devices in a mesh: path: 16 (over y_hi, x), shard: 32 (over y_lo, z, core).
Axes of the slice: x: 4, y: 8 (y_hi: 4, y_lo: 2; y = y_hi * 2 + y_lo), z: 8, core: 2. Of those that a mesh axis runs over, the one named last changes fastest.
Arguments:
- tokens: bfloat16 [8192, 2048], P('path', 'shard'), may hold values from -6 to 6
- cotangent: bfloat16 [8192, 2048], P('path', 'shard'), may hold values from -6 to 6
- weights: bfloat16 [16, 4, 3, 7168, 128], P('path', None, None, 'shard'), may hold values from -0.125 to 0.125
- momentum: float32 [16, 4, 3, 7168, 128], P('path', None, None, 'shard'), may hold values from -4 to 4
- cluster: int32 [64], replicated, may hold values from 0 to 15, as said below
- path_module: int32 [16, 1], replicated, may hold values from 0 to 3
- owner: int32 [4, 16], replicated, may hold values from 0 to 15, each once within a row
Outputs:
- input_grad: bfloat16 [8192, 2048], P('path', 'shard')
- new_weights: float32 [16, 4, 3, 7168, 128], P('path', None, None, 'shard')
- new_momentum: float32 [16, 4, 3, 7168, 128], P('path', None, None, 'shard')
The draws below stay inside these ranges and needn't reach their ends.
Inputs may be any that keep to these rules, and one draw needn't show every extreme that they name: `cluster`: every path receives exactly 4 blocks; each path sends exactly one of its 4 blocks to each of 4 distinct paths (possibly itself). `path_module`: every module is used by at least one path. `owner`: each row names every path once.
All inputs are finite; a program needn't handle non-finite values.
Results may differ from the reference program's by a relative error of at most 0.005.
Values may be sent and summed in bfloat16 or wider, within the bound.
No kernel may reach another device: no remote copies, remote signals or barrier semaphores. Data moves between devices by JAX's collectives and lax.ppermute only.
A program may use at most 64 MiB of HBM per device.

```python
import jax
import jax.numpy as jnp
from jax import lax

D = 2048
FF = 7168
MODULES = 4
BLK = 128
TB = 4
DT = 128
ROWS = 8192
N_PATH = 16


def draw_cluster(key, part):
    key = jax.random.fold_in(key, 11)
    keys = jax.random.split(key, 3)
    relabel = jax.random.permutation(keys[0], N_PATH)
    offsets = jax.random.permutation(keys[1], N_PATH)
    placed = jax.vmap(lambda one_key: jax.random.permutation(one_key, TB))(jax.random.split(keys[2], N_PATH))
    target = relabel[(offsets[:, None] + placed) % N_PATH]
    return target.reshape(N_PATH * TB).astype(jnp.int32)


def levels(rng, shape, cuts, low, largest):
    def one(axis_at, parts):
        steps = jax.random.uniform(jax.random.fold_in(jax.random.fold_in(rng, 6), axis_at), (parts,), jnp.float32, low / len(cuts), largest / len(cuts))
        return jnp.repeat(jnp.exp(steps), shape[axis_at] // parts).reshape((-1,) + (1,) * (len(shape) - axis_at - 1))

    gain = one(*cuts[0])
    for cut in cuts[1:]:
        gain = gain * one(*cut)
    return gain


def different_ones(own_key, rows, number_of, top, lift):
    sequence = jax.random.permutation(jax.random.fold_in(own_key, 1), number_of)
    pull = sequence
    for power in range(3):
        pull = pull * pull // number_of
    pull = pull * lift // number_of
    lots = jax.random.randint(jax.random.fold_in(own_key, 2), (rows, number_of), 0, 4096) + pull
    holders = jax.random.permutation(jax.random.fold_in(own_key, 3), rows)[jnp.arange(number_of) % rows]
    lots = jnp.where(jnp.arange(rows)[:, None] == holders[None, :], 1 << 14, lots)
    score = lots * number_of + jnp.arange(number_of)
    return lax.top_k(score.astype(jnp.int32), top)[1].astype(jnp.int32)


def gaussian(rng, extent, spread, most, pieces=(), held_as=jnp.bfloat16):
    factor_of = levels(rng, extent, pieces, -0.22, 0.18) if pieces else 1.0
    array = jax.random.normal(rng, extent, jnp.float32) * spread * factor_of
    return jnp.minimum(jnp.maximum(array, -most), most).astype(held_as)


def setup_inputs(seed: int = 0) -> dict:
    key_list = jax.random.split(jax.random.key(seed), 8)
    return {
        "tokens": gaussian(key_list[0], (ROWS, D), 1.0, 6.0, ((0, 16), (1, 32))),
        "cotangent": gaussian(key_list[1], (ROWS, D), 1.0, 6.0, ((0, 16), (1, 32))),
        "weights": gaussian(key_list[2], (N_PATH, MODULES, 3, FF, DT), D ** -0.5, 0.125, ((0, 16), (3, 32))),
        "momentum": gaussian(key_list[3], (N_PATH, MODULES, 3, FF, DT), 0.5, 4.0, ((0, 16), (3, 32)), jnp.float32),
        "cluster": draw_cluster(jax.random.fold_in(key_list[7], 71), 0),
        "path_module": different_ones(key_list[5], N_PATH, MODULES, 1, 4096),
        "owner": jax.vmap(lambda own: jax.random.permutation(own, N_PATH))(jax.random.split(key_list[6], MODULES)).reshape((MODULES, N_PATH)).astype(jnp.int32),
    }


MU = 0.9
LR_INNER = 0.05
LR_OUTER = 0.02


def contract_rows(left, right):
    return lax.dot_general(left, right, (((0,), (0,)), ((), ())), preferred_element_type=jnp.float32)


def reference(tokens, cotangent, weights, momentum, cluster, path_module, owner):
    modules_of = path_module[:, 0]
    module_ids = jnp.arange(MODULES, dtype=jnp.int32)
    order = jnp.argsort(cluster, stable=True).astype(jnp.int32)
    whole = weights[owner, module_ids[:, None]]
    token_blocks = tokens.reshape(N_PATH * TB, BLK * D)
    cot_blocks = cotangent.reshape(N_PATH * TB, BLK * D)

    def one_path(total, path):
        chosen = lax.dynamic_slice_in_dim(order, path * TB, TB)
        rows = jnp.take(token_blocks, chosen, axis=0).reshape(TB * BLK, D)
        cot_rows = jnp.take(cot_blocks, chosen, axis=0).reshape(TB * BLK, D)
        module = modules_of[path]
        tiles = lax.dynamic_index_in_dim(whole, module, 0, keepdims=False)
        w_gate = tiles[:, 0].transpose(0, 2, 1).reshape(D, FF)
        w_up = tiles[:, 1].transpose(0, 2, 1).reshape(D, FF)
        w_down = tiles[:, 2].transpose(0, 2, 1).reshape(D, FF)
        gate_pre = jnp.dot(rows, w_gate, preferred_element_type=jnp.float32)
        up_pre = jnp.dot(rows, w_up, preferred_element_type=jnp.float32)
        gate_sigmoid = jax.nn.sigmoid(gate_pre)
        gate_act = gate_pre * gate_sigmoid
        hidden = (gate_act * up_pre).astype(jnp.bfloat16)
        hidden_grad = jnp.dot(cot_rows, w_down, preferred_element_type=jnp.float32)
        gate_grad = (hidden_grad * up_pre * gate_sigmoid * (1.0 + gate_pre * (1.0 - gate_sigmoid))).astype(jnp.bfloat16)
        up_grad = (hidden_grad * gate_act).astype(jnp.bfloat16)
        grad_gate = contract_rows(rows, gate_grad)
        grad_up = contract_rows(rows, up_grad)
        grad_down = contract_rows(cot_rows, hidden)
        back = lax.dot_general(gate_grad, w_gate, (((1,), (1,)), ((), ())), preferred_element_type=jnp.float32)
        back = back + lax.dot_general(up_grad, w_up, (((1,), (1,)), ((), ())), preferred_element_type=jnp.float32)
        input_grad = back.astype(jnp.bfloat16)
        grads = jnp.stack([grad_gate, grad_up, grad_down])
        delta = (LR_INNER * grads).astype(jnp.bfloat16).astype(jnp.float32)
        total = total.at[module].add(delta)
        return total, input_grad

    start = jnp.zeros((MODULES, 3, D, FF), jnp.float32)
    total, input_grads = lax.scan(one_path, start, jnp.arange(N_PATH, dtype=jnp.int32))
    counts = jnp.sum((modules_of[None, :] == module_ids[:, None]).astype(jnp.float32), axis=1)
    mean_delta = total / counts[:, None, None, None]
    mean_tiles = mean_delta.reshape(MODULES, 3, N_PATH, D // N_PATH, FF).transpose(0, 2, 1, 4, 3)
    moment_tiles = momentum[owner, module_ids[:, None]]
    new_moment = MU * moment_tiles + mean_tiles
    new_tiles = whole.astype(jnp.float32) - LR_OUTER * (mean_tiles + MU * new_moment)
    placed_weights = jnp.zeros(weights.shape, jnp.float32).at[owner, module_ids[:, None]].set(new_tiles)
    placed_moment = jnp.zeros(momentum.shape, jnp.float32).at[owner, module_ids[:, None]].set(new_moment)
    return input_grads.reshape(N_PATH * TB * BLK, D), placed_weights, placed_moment
```

```python
import jax
import jax.numpy as jnp
from jax import lax
from jax.experimental import pallas as pl
from jax.experimental.pallas import tpu as pltpu
from jax.sharding import Mesh, PartitionSpec as P

MODULES = 4
BLK = 128
MU = 0.9
LR_INNER = 0.05
LR_OUTER = 0.02

PATH = ("yh", "x")
SHARD = ("yl", "z", "c")
CHIPS = ("yl", "z")
VMEM_LIMIT = 48 * 1024 * 1024


def grads_kernel(tile_ref, core_ref, w_ref, mine_ref, other_ref, delta_ref, dgu_ref, xp, yp, g_s, u_s, d_s, h_s):
    owners, _, units, width = w_ref.shape
    core = core_ref[0]

    def place(o, carry):
        j = pl.multiple_of(tile_ref[o] * width, width)
        to = pl.multiple_of(o * width, width)
        a = mine_ref[pl.ds(j, width), :]
        b = other_ref[pl.ds(j, width), :]
        xp[pl.ds(to, width), :] = jnp.where(core == 0, a, b)
        yp[pl.ds(to, width), :] = jnp.where(core == 0, b, a)
        return carry

    lax.fori_loop(0, owners, place, 0)

    def matrix(k):
        return jnp.concatenate([w_ref[o, k] for o in range(owners)], axis=1)

    g_s[...] = jnp.dot(matrix(0), xp[...], preferred_element_type=jnp.float32)
    u_s[...] = jnp.dot(matrix(1), xp[...], preferred_element_type=jnp.float32)
    d_s[...] = jnp.dot(matrix(2), yp[...], preferred_element_type=jnp.float32)
    step = 32

    def act(i, carry):
        at = pl.multiple_of(i * step, step)
        rows = pl.ds(at, step)
        gate = g_s[rows, :]
        up = u_s[rows, :]
        dh = d_s[rows, :]
        sig = jax.nn.sigmoid(gate)
        silu = gate * sig
        h_s[rows, :] = (silu * up).astype(jnp.bfloat16)
        dgu_ref[rows, :] = (dh * up * sig * (1.0 + gate * (1.0 - sig))).astype(jnp.bfloat16)
        dgu_ref[pl.ds(pl.multiple_of(units + at, step), step), :] = (dh * silu).astype(jnp.bfloat16)
        return carry

    lax.fori_loop(0, units // step, act, 0)
    nt = (((1,), (1,)), ((), ()))

    def back(p, carry):
        rows = pl.ds(pl.multiple_of(p * 2 * width, 2 * width), 2 * width)
        gu = LR_INNER * lax.dot_general(dgu_ref[...], xp[rows, :], nt, preferred_element_type=jnp.float32)
        dn = LR_INNER * lax.dot_general(h_s[...], yp[rows, :], nt, preferred_element_type=jnp.float32)
        gu = gu.astype(jnp.bfloat16)
        dn = dn.astype(jnp.bfloat16)
        for half in range(2):
            lanes = slice(half * width, (half + 1) * width)
            delta_ref[2 * p + half, 0] = gu[:units, lanes]
            delta_ref[2 * p + half, 1] = gu[units:, lanes]
            delta_ref[2 * p + half, 2] = dn[:, lanes]
        return carry

    lax.fori_loop(0, owners // 2, back, 0)


def input_kernel(tile_ref, w_ref, dgu_ref, dx_ref):
    owners, _, units, width = w_ref.shape
    half = width // 2

    def one(o, carry):
        w = w_ref[o, 0:2].reshape(2 * units, width)
        part = lax.dot_general(w, dgu_ref[...], (((0,), (0,)), ((), ())), preferred_element_type=jnp.float32)
        j = tile_ref[o]
        dx_ref[0, j] = part[:half]
        dx_ref[1, j] = part[half:]
        return carry

    lax.fori_loop(0, owners, one, 0)


def grads(tile_of, core, w, mine, other):
    owners, _, units, width = w.shape
    rows = mine.shape[1]
    smem = pl.BlockSpec(memory_space=pltpu.SMEM)
    vmem = pl.BlockSpec(memory_space=pltpu.VMEM)
    return pl.pallas_call(
        grads_kernel,
        out_shape=(
            jax.ShapeDtypeStruct(w.shape, jnp.bfloat16),
            jax.ShapeDtypeStruct((2 * units, rows), jnp.bfloat16),
        ),
        in_specs=[smem, smem, vmem, vmem, vmem],
        out_specs=(vmem, vmem),
        scratch_shapes=[
            pltpu.VMEM(mine.shape, jnp.bfloat16),
            pltpu.VMEM(mine.shape, jnp.bfloat16),
            pltpu.VMEM((units, rows), jnp.float32),
            pltpu.VMEM((units, rows), jnp.float32),
            pltpu.VMEM((units, rows), jnp.float32),
            pltpu.VMEM((units, rows), jnp.bfloat16),
        ],
        compiler_params=pltpu.CompilerParams(vmem_limit_bytes=VMEM_LIMIT),
        cost_estimate=pl.CostEstimate(
            flops=12 * units * rows * owners * width, bytes_accessed=12 * 2**20, transcendentals=units * rows
        ),
        name="grads",
    )(tile_of, core, w, mine, other)


def input_partial(tile_of, w, dgu):
    owners, _, units, width = w.shape
    rows = dgu.shape[1]
    smem = pl.BlockSpec(memory_space=pltpu.SMEM)
    vmem = pl.BlockSpec(memory_space=pltpu.VMEM)
    return pl.pallas_call(
        input_kernel,
        out_shape=jax.ShapeDtypeStruct((2, owners, width // 2, rows), jnp.float32),
        in_specs=[smem, vmem, vmem],
        out_specs=vmem,
        compiler_params=pltpu.CompilerParams(vmem_limit_bytes=VMEM_LIMIT),
        cost_estimate=pl.CostEstimate(
            flops=4 * units * rows * owners * width, bytes_accessed=8 * 2**20, transcendentals=0
        ),
        name="input_partial",
    )(tile_of, w, dgu)


def pick(array, index):
    return array.at[index].get(mode="promise_in_bounds")


def body(tokens, cotangent, weights, momentum, cluster, path_module, owner):
    paths = lax.axis_size(PATH)
    here = lax.axis_index(PATH)
    core = lax.axis_index("c")
    modules_of = path_module[:, 0]
    path_ids = jnp.arange(paths, dtype=jnp.int32)
    blocks = tokens.shape[0] // BLK
    cols = tokens.shape[1]
    owned = weights[0]

    send_w = pick(owned, modules_of)
    recv_w = lax.all_to_all(send_w, PATH, split_axis=0, concat_axis=0, tiled=True)

    def feature_major(array):
        return array.reshape(blocks, BLK, cols).transpose(0, 2, 1)

    both = jnp.stack([feature_major(tokens), feature_major(cotangent)], axis=1)
    own_dest = lax.dynamic_slice_in_dim(cluster, here * blocks, blocks)
    goes = own_dest[None, :] == path_ids[:, None]
    block_ids = jnp.arange(blocks, dtype=jnp.int32)
    send_x = pick(both, jnp.sum(jnp.where(goes, block_ids[None, :], 0), axis=1))
    recv_x = lax.all_to_all(
        send_x.reshape(paths * 2, cols, BLK), PATH + ("c",), split_axis=0, concat_axis=0, tiled=True
    ).reshape(paths, 2, cols, BLK)
    has = jnp.any(cluster.reshape(paths, blocks) == here, axis=1)
    before = jnp.sum((has[None, :] & (path_ids[None, :] < path_ids[:, None])).astype(jnp.int32), axis=1)
    comes = has[None, :] & (before[None, :] == block_ids[:, None])
    sources = jnp.sum(jnp.where(comes, path_ids[None, :], 0), axis=1)
    piece = pick(recv_x, sources).transpose(1, 2, 0, 3).reshape(2 * cols, blocks * BLK)

    mine = lax.all_gather(piece, CHIPS, axis=0, tiled=True)
    swap = [(0, 1), (1, 0)]
    other = lax.ppermute(mine, "c", swap)

    owner_row = owner[modules_of[here]]
    tile_of = jnp.sum(jnp.where(owner_row[None, :] == path_ids[:, None], path_ids[None, :], 0), axis=1)
    delta, dgu = grads(tile_of, core.reshape(1), recv_w, mine, other)
    recv_delta = lax.all_to_all(delta, PATH, split_axis=0, concat_axis=0, tiled=True)

    dx = input_partial(tile_of, recv_w, dgu)
    keep = lax.dynamic_index_in_dim(dx, core, 0, keepdims=False)
    give = lax.dynamic_index_in_dim(dx, 1 - core, 0, keepdims=False)
    chip_dx = keep + lax.ppermute(give, "c", swap)
    chip_dx = chip_dx.reshape(paths * cols, blocks * BLK)
    total = lax.psum_scatter(chip_dx, CHIPS, scatter_dimension=0, tiled=True)
    input_grad = total.astype(jnp.bfloat16).T

    member = modules_of[None, :] == jnp.arange(MODULES, dtype=jnp.int32)[:, None]
    counts = jnp.sum(member.astype(jnp.float32), axis=1)
    sums = jnp.einsum(
        "mq,qabc->mabc", member.astype(jnp.bfloat16), recv_delta, preferred_element_type=jnp.float32
    )
    mean_delta = sums / counts[:, None, None, None]
    new_moment = MU * momentum[0] + mean_delta
    new_tiles = owned.astype(jnp.float32) - LR_OUTER * (mean_delta + MU * new_moment)
    return (input_grad, new_tiles[None], new_moment[None])


def solution(mesh):
    fine = Mesh(mesh.devices.reshape(4, 4, 2, 8, 2), PATH + SHARD)
    tiles = P(PATH, None, None, SHARD, None)
    return jax.shard_map(
        body,
        mesh=fine,
        in_specs=(P(PATH, SHARD), P(PATH, SHARD), tiles, tiles, P(), P(), P()),
        out_specs=(P(PATH, SHARD), tiles, tiles),
        check_vma=False,
    )
```

```python
import jax
import jax.numpy as jnp
from jax import lax
from jax.experimental import pallas as pl
from jax.experimental.pallas import tpu as pltpu
from jax.sharding import Mesh, PartitionSpec as P

MODULES = 4
BLK = 128
MU = 0.9
LR_INNER = 0.05
LR_OUTER = 0.02

PATH = ("yh", "x")
SHARD = ("yl", "z", "c")
VMEM_LIMIT = 48 * 1024 * 1024


def grads_kernel(tile_ref, core_ref, w_ref, mine_ref, other_ref, delta_ref, dgu_ref, xp, yp, g_s, u_s, d_s, h_s):
    owners, _, units, width = w_ref.shape
    core = core_ref[0]

    def place(o, carry):
        j = pl.multiple_of(tile_ref[o] * width, width)
        to = pl.multiple_of(o * width, width)
        a = mine_ref[pl.ds(j, width), :]
        b = other_ref[pl.ds(j, width), :]
        xp[pl.ds(to, width), :] = jnp.where(core == 0, a, b)
        yp[pl.ds(to, width), :] = jnp.where(core == 0, b, a)
        return carry

    lax.fori_loop(0, owners, place, 0)

    def matrix(k):
        return jnp.concatenate([w_ref[o, k] for o in range(owners)], axis=1)

    g_s[...] = jnp.dot(matrix(0), xp[...], preferred_element_type=jnp.float32)
    u_s[...] = jnp.dot(matrix(1), xp[...], preferred_element_type=jnp.float32)
    d_s[...] = jnp.dot(matrix(2), yp[...], preferred_element_type=jnp.float32)
    step = 32

    def act(i, carry):
        at = pl.multiple_of(i * step, step)
        rows = pl.ds(at, step)
        gate = g_s[rows, :]
        up = u_s[rows, :]
        dh = d_s[rows, :]
        sig = jax.nn.sigmoid(gate)
        silu = gate * sig
        h_s[rows, :] = (silu * up).astype(jnp.bfloat16)
        dgu_ref[rows, :] = (dh * up * sig * (1.0 + gate * (1.0 - sig))).astype(jnp.bfloat16)
        dgu_ref[pl.ds(pl.multiple_of(units + at, step), step), :] = (dh * silu).astype(jnp.bfloat16)
        return carry

    lax.fori_loop(0, units // step, act, 0)
    nt = (((1,), (1,)), ((), ()))

    def back(p, carry):
        rows = pl.ds(pl.multiple_of(p * 2 * width, 2 * width), 2 * width)
        gu = LR_INNER * lax.dot_general(dgu_ref[...], xp[rows, :], nt, preferred_element_type=jnp.float32)
        dn = LR_INNER * lax.dot_general(h_s[...], yp[rows, :], nt, preferred_element_type=jnp.float32)
        gu = gu.astype(jnp.bfloat16)
        dn = dn.astype(jnp.bfloat16)
        for half in range(2):
            lanes = slice(half * width, (half + 1) * width)
            delta_ref[2 * p + half, 0] = gu[:units, lanes]
            delta_ref[2 * p + half, 1] = gu[units:, lanes]
            delta_ref[2 * p + half, 2] = dn[:, lanes]
        return carry

    lax.fori_loop(0, owners // 2, back, 0)


def input_kernel(slot_ref, core_ref, w_ref, dgu_ref, keep_ref, give_ref):
    owners, _, units, width = w_ref.shape
    half = width // 2
    core = core_ref[0]

    def one(o, carry):
        w = w_ref[o, 0:2].reshape(2 * units, width)
        part = lax.dot_general(w, dgu_ref[...], (((0,), (0,)), ((), ())), preferred_element_type=jnp.float32)
        j = slot_ref[o]
        low, high = part[:half], part[half:]
        keep_ref[j] = jnp.where(core == 0, low, high)
        give_ref[j] = jnp.where(core == 0, high, low).astype(jnp.bfloat16)
        return carry

    lax.fori_loop(0, owners, one, 0)


def pair_kernel(keep_ref, came_ref, own_ref, *out_refs):
    for k in range(len(out_refs) + 1):
        at = slice(2 * k, 2 * k + 2)
        total = keep_ref[at] + came_ref[at].astype(jnp.float32)
        if k == 0:
            own_ref[...] = total
        else:
            out_refs[k - 1][...] = total.astype(jnp.bfloat16)


def update_kernel(module_ref, count_ref, delta_ref, weight_ref, momentum_ref, new_w_ref, new_m_ref, acc):
    modules = weight_ref.shape[0]
    acc[...] = jnp.zeros_like(acc)

    def add(q, carry):
        m = module_ref[q]
        acc[m] += delta_ref[q, 0].astype(jnp.float32)
        return carry

    lax.fori_loop(0, delta_ref.shape[0], add, 0)
    for m in range(modules):
        mean = acc[m] / count_ref[m]
        moment = MU * momentum_ref[m, 0] + mean
        new_m_ref[m, 0] = moment
        new_w_ref[m, 0] = weight_ref[m, 0].astype(jnp.float32) - LR_OUTER * (mean + MU * moment)


def grads(tile_of, core, w, mine, other):
    owners, _, units, width = w.shape
    rows = mine.shape[1]
    smem = pl.BlockSpec(memory_space=pltpu.SMEM)
    vmem = pl.BlockSpec(memory_space=pltpu.VMEM)
    return pl.pallas_call(
        grads_kernel,
        out_shape=(
            jax.ShapeDtypeStruct(w.shape, jnp.bfloat16),
            jax.ShapeDtypeStruct((2 * units, rows), jnp.bfloat16),
        ),
        in_specs=[smem, smem, vmem, vmem, vmem],
        out_specs=(vmem, vmem),
        scratch_shapes=[
            pltpu.VMEM(mine.shape, jnp.bfloat16),
            pltpu.VMEM(mine.shape, jnp.bfloat16),
            pltpu.VMEM((units, rows), jnp.float32),
            pltpu.VMEM((units, rows), jnp.float32),
            pltpu.VMEM((units, rows), jnp.float32),
            pltpu.VMEM((units, rows), jnp.bfloat16),
        ],
        compiler_params=pltpu.CompilerParams(vmem_limit_bytes=VMEM_LIMIT),
        cost_estimate=pl.CostEstimate(
            flops=12 * units * rows * owners * width, bytes_accessed=12 * 2**20, transcendentals=units * rows
        ),
        name="grads",
    )(tile_of, core, w, mine, other)


def input_partial(slot_of, core, w, dgu):
    owners, _, units, width = w.shape
    rows = dgu.shape[1]
    smem = pl.BlockSpec(memory_space=pltpu.SMEM)
    vmem = pl.BlockSpec(memory_space=pltpu.VMEM)
    shape = (owners, width // 2, rows)
    return pl.pallas_call(
        input_kernel,
        out_shape=(jax.ShapeDtypeStruct(shape, jnp.float32), jax.ShapeDtypeStruct(shape, jnp.bfloat16)),
        in_specs=[smem, smem, vmem, vmem],
        out_specs=(vmem, vmem),
        compiler_params=pltpu.CompilerParams(vmem_limit_bytes=VMEM_LIMIT),
        cost_estimate=pl.CostEstimate(flops=1000, bytes_accessed=1000, transcendentals=0),
        name="input_partial",
    )(slot_of, core, w, dgu)


def pair_sums(keep, came):
    tiles, feats, rows = keep.shape
    vmem = pl.BlockSpec(memory_space=pltpu.VMEM)
    part = (2, feats, rows)
    steps = tiles // 2
    return pl.pallas_call(
        pair_kernel,
        out_shape=(jax.ShapeDtypeStruct(part, jnp.float32),)
        + (jax.ShapeDtypeStruct(part, jnp.bfloat16),) * (steps - 1),
        in_specs=[vmem, vmem],
        out_specs=(vmem,) * steps,
        compiler_params=pltpu.CompilerParams(vmem_limit_bytes=VMEM_LIMIT),
        cost_estimate=pl.CostEstimate(flops=1000, bytes_accessed=1000, transcendentals=0),
        name="pair_sums",
    )(keep, came)


def update(modules_of, counts, delta, owned, momentum):
    paths = delta.shape[0]
    modules, mats, units, width = owned.shape
    rows = units // 2
    smem = pl.BlockSpec(memory_space=pltpu.SMEM)
    tile = pl.BlockSpec((modules, 1, rows, width), lambda k, i: (0, k, i, 0))
    return pl.pallas_call(
        update_kernel,
        grid=(mats, units // rows),
        out_shape=(jax.ShapeDtypeStruct(momentum.shape, jnp.float32),) * 2,
        in_specs=[
            smem,
            smem,
            pl.BlockSpec((paths, 1, rows, width), lambda k, i: (0, k, i, 0)),
            tile,
            tile,
        ],
        out_specs=(tile, tile),
        scratch_shapes=[pltpu.VMEM((modules, rows, width), jnp.float32)],
        compiler_params=pltpu.CompilerParams(vmem_limit_bytes=VMEM_LIMIT),
        cost_estimate=pl.CostEstimate(flops=10**6, bytes_accessed=8 * 2**20, transcendentals=0),
        name="update",
    )(modules_of, counts, delta, owned, momentum)


def pick(array, index):
    return array.at[index].get(mode="promise_in_bounds")


def turn(size, k):
    return [(i, (i + k) % size) for i in range(size)]


def ring_gather(piece):
    depth = lax.axis_size("z")
    beside = lax.ppermute(piece, "yl", [(0, 1), (1, 0)])
    first = lax.axis_index("yl") == 0
    pair = jnp.concatenate([jnp.where(first, piece, beside), jnp.where(first, beside, piece)], axis=0)
    half = piece.shape[0]
    up = down = pair
    parts = [pair]
    at = [0] * depth
    for k in range(1, depth // 2):
        up = lax.ppermute(up, "z", turn(depth, 1))
        down = lax.ppermute(down, "z", turn(depth, -1))
        at[depth - k] = len(parts)
        at[k] = len(parts) + 1
        parts += [up, down]
    at[depth // 2] = len(parts)
    parts.append(lax.ppermute(up[:half], "z", turn(depth, 1)))
    parts.append(lax.ppermute(down[half:], "z", turn(depth, -1)))
    return jnp.concatenate(parts, axis=0), at


def body(tokens, cotangent, weights, momentum, cluster, path_module, owner):
    paths = lax.axis_size(PATH)
    here = lax.axis_index(PATH)
    core = lax.axis_index("c")
    modules_of = path_module[:, 0]
    path_ids = jnp.arange(paths, dtype=jnp.int32)
    blocks = tokens.shape[0] // BLK
    cols = tokens.shape[1]
    owned = weights[0]

    send_w = pick(owned, modules_of)
    recv_w = lax.all_to_all(send_w, PATH, split_axis=0, concat_axis=0, tiled=True)

    def feature_major(array):
        return array.reshape(blocks, BLK, cols).transpose(0, 2, 1)

    both = jnp.stack([feature_major(tokens), feature_major(cotangent)], axis=1)
    own_dest = lax.dynamic_slice_in_dim(cluster, here * blocks, blocks)
    goes = own_dest[None, :] == path_ids[:, None]
    block_ids = jnp.arange(blocks, dtype=jnp.int32)
    send_x = pick(both, jnp.sum(jnp.where(goes, block_ids[None, :], 0), axis=1))
    recv_x = lax.all_to_all(
        send_x.reshape(paths * 2, cols, BLK), PATH + ("c",), split_axis=0, concat_axis=0, tiled=True
    ).reshape(paths, 2, cols, BLK)
    has = jnp.any(cluster.reshape(paths, blocks) == here, axis=1)
    before = jnp.sum((has[None, :] & (path_ids[None, :] < path_ids[:, None])).astype(jnp.int32), axis=1)
    comes = has[None, :] & (before[None, :] == block_ids[:, None])
    sources = jnp.sum(jnp.where(comes, path_ids[None, :], 0), axis=1)
    piece = pick(recv_x, sources).transpose(1, 2, 0, 3).reshape(2 * cols, blocks * BLK)

    mine, at = ring_gather(piece)
    swap = [(0, 1), (1, 0)]
    other = lax.ppermute(mine, "c", swap)

    owner_row = owner[modules_of[here]]
    tile_of = jnp.sum(jnp.where(owner_row[None, :] == path_ids[:, None], path_ids[None, :], 0), axis=1)
    z = lax.axis_index("z")
    depth = lax.axis_size("z")
    away = (tile_of % depth - z) % depth
    side = tile_of // depth
    place = jnp.sum(jnp.where(away[:, None] == jnp.arange(depth)[None, :], jnp.array(at, jnp.int32)[None, :], 0), axis=1)
    core_id = core.reshape(1)
    delta, dgu = grads(place * 2 + side, core_id, recv_w, mine, other)
    recv_delta = lax.all_to_all(delta, PATH, split_axis=0, concat_axis=0, tiled=True)

    keep, give = input_partial(away * 2 + side, core_id, recv_w, dgu)
    sums = pair_sums(keep, lax.ppermute(give, "c", swap))
    came = [lax.ppermute(sums[k], "z", turn(depth, k)) for k in range(1, depth)]
    total = sums[0]
    for part in came:
        total = total + part.astype(jnp.float32)
    yl = lax.axis_index("yl")
    theirs = lax.ppermute(lax.dynamic_index_in_dim(total, 1 - yl, 0, keepdims=False), "yl", swap)
    total = lax.dynamic_index_in_dim(total, yl, 0, keepdims=False) + theirs
    input_grad = total.astype(jnp.bfloat16).T

    member = modules_of[None, :] == jnp.arange(MODULES, dtype=jnp.int32)[:, None]
    counts = jnp.sum(member.astype(jnp.float32), axis=1)
    new_tiles, new_moment = update(modules_of, counts, recv_delta, owned, momentum[0])
    return (input_grad, new_tiles[None], new_moment[None])


def solution(mesh):
    fine = Mesh(mesh.devices.reshape(4, 4, 2, 8, 2), PATH + SHARD)
    tiles = P(PATH, None, None, SHARD, None)
    return jax.shard_map(
        body,
        mesh=fine,
        in_specs=(P(PATH, SHARD), P(PATH, SHARD), tiles, tiles, P(), P(), P()),
        out_specs=(P(PATH, SHARD), tiles, tiles),
        check_vma=False,
    )
```

```python
import jax
import jax.numpy as jnp
from jax import lax
from jax.experimental import pallas as pl
from jax.experimental.pallas import tpu as pltpu
from jax.sharding import Mesh, PartitionSpec as P

MODULES = 4
BLK = 128
MU = 0.9
LR_INNER = 0.05
LR_OUTER = 0.02

PATH = ("yh", "x")
SHARD = ("yl", "z", "c")
VMEM_LIMIT = 24 * 1024 * 1024


def place_kernel(place_ref, core_ref, mine_ref, other_ref, xp_ref, yp_ref):
    owners = place_ref.shape[0]
    width = mine_ref.shape[0] // owners
    first = core_ref[0] == 0

    def one(o, carry):
        here = pl.ds(pl.multiple_of(place_ref[o] * width, width), width)
        to = pl.ds(pl.multiple_of(o * width, width), width)
        a = mine_ref[here, :]
        b = other_ref[here, :]
        xp_ref[to, :] = jnp.where(first, a, b)
        yp_ref[to, :] = jnp.where(first, b, a)
        return carry

    lax.fori_loop(0, owners, one, 0)


def grads_kernel(w_ref, xp, yp, delta_ref, dgu_ref, g_s, u_s, d_s, h_s):
    owners, _, units, width = w_ref.shape

    def matrix(k):
        return jnp.concatenate([w_ref[o, k] for o in range(owners)], axis=1)

    g_s[...] = jnp.dot(matrix(0), xp[...], preferred_element_type=jnp.float32)
    u_s[...] = jnp.dot(matrix(1), xp[...], preferred_element_type=jnp.float32)
    d_s[...] = jnp.dot(matrix(2), yp[...], preferred_element_type=jnp.float32)
    step = 32

    def act(i, carry):
        at = pl.multiple_of(i * step, step)
        rows = pl.ds(at, step)
        gate = g_s[rows, :]
        up = u_s[rows, :]
        dh = d_s[rows, :]
        sig = jax.nn.sigmoid(gate)
        silu = gate * sig
        h_s[rows, :] = (silu * up).astype(jnp.bfloat16)
        dgu_ref[rows, :] = (dh * up * sig * (1.0 + gate * (1.0 - sig))).astype(jnp.bfloat16)
        dgu_ref[pl.ds(pl.multiple_of(units + at, step), step), :] = (dh * silu).astype(jnp.bfloat16)
        return carry

    lax.fori_loop(0, units // step, act, 0)
    nt = (((1,), (1,)), ((), ()))

    def back(p, carry):
        rows = pl.ds(pl.multiple_of(p * 2 * width, 2 * width), 2 * width)
        gu = LR_INNER * lax.dot_general(dgu_ref[...], xp[rows, :], nt, preferred_element_type=jnp.float32)
        dn = LR_INNER * lax.dot_general(h_s[...], yp[rows, :], nt, preferred_element_type=jnp.float32)
        gu = gu.astype(jnp.bfloat16)
        dn = dn.astype(jnp.bfloat16)
        for half in range(2):
            lanes = slice(half * width, (half + 1) * width)
            delta_ref[2 * p + half, 0] = gu[:units, lanes]
            delta_ref[2 * p + half, 1] = gu[units:, lanes]
            delta_ref[2 * p + half, 2] = dn[:, lanes]
        return carry

    lax.fori_loop(0, owners // 2, back, 0)


def input_kernel(slot_ref, core_ref, w_ref, dgu_ref, keep_ref, give_ref):
    owners, _, units, width = w_ref.shape
    half = width // 2
    core = core_ref[0]

    def one(o, carry):
        w = w_ref[o, 0:2].reshape(2 * units, width)
        part = lax.dot_general(w, dgu_ref[...], (((0,), (0,)), ((), ())), preferred_element_type=jnp.float32)
        j = slot_ref[o]
        low, high = part[:half], part[half:]
        keep_ref[j] = jnp.where(core == 0, low, high)
        give_ref[j] = jnp.where(core == 0, high, low).astype(jnp.bfloat16)
        return carry

    lax.fori_loop(0, owners, one, 0)


def pair_kernel(keep_ref, came_ref, own_ref, *out_refs):
    for k in range(len(out_refs) + 1):
        at = slice(2 * k, 2 * k + 2)
        total = keep_ref[at] + came_ref[at].astype(jnp.float32)
        if k == 0:
            own_ref[...] = total
        else:
            out_refs[k - 1][...] = total.astype(jnp.bfloat16)


def update_kernel(module_ref, count_ref, delta_ref, weight_ref, momentum_ref, new_w_ref, new_m_ref, acc):
    modules = weight_ref.shape[0]
    acc[...] = jnp.zeros_like(acc)

    def add(q, carry):
        m = module_ref[q]
        acc[m] += delta_ref[q, 0].astype(jnp.float32)
        return carry

    lax.fori_loop(0, delta_ref.shape[0], add, 0)
    for m in range(modules):
        mean = acc[m] / count_ref[m]
        moment = MU * momentum_ref[m, 0] + mean
        new_m_ref[m, 0] = moment
        new_w_ref[m, 0] = weight_ref[m, 0].astype(jnp.float32) - LR_OUTER * (mean + MU * moment)


def in_owner_order(place, core, mine, other):
    smem = pl.BlockSpec(memory_space=pltpu.SMEM)
    vmem = pl.BlockSpec(memory_space=pltpu.VMEM)
    return pl.pallas_call(
        place_kernel,
        out_shape=(jax.ShapeDtypeStruct(mine.shape, mine.dtype),) * 2,
        in_specs=[smem, smem, vmem, vmem],
        out_specs=(vmem, vmem),
        compiler_params=pltpu.CompilerParams(vmem_limit_bytes=VMEM_LIMIT),
        cost_estimate=pl.CostEstimate(flops=1000, bytes_accessed=1000, transcendentals=0),
        name="in_owner_order",
    )(place, core, mine, other)


def grads(w, xp, yp):
    owners, _, units, width = w.shape
    rows = xp.shape[1]
    vmem = pl.BlockSpec(memory_space=pltpu.VMEM)
    return pl.pallas_call(
        grads_kernel,
        out_shape=(
            jax.ShapeDtypeStruct(w.shape, jnp.bfloat16),
            jax.ShapeDtypeStruct((2 * units, rows), jnp.bfloat16),
        ),
        in_specs=[vmem, vmem, vmem],
        out_specs=(vmem, vmem),
        scratch_shapes=[
            pltpu.VMEM((units, rows), jnp.float32),
            pltpu.VMEM((units, rows), jnp.float32),
            pltpu.VMEM((units, rows), jnp.float32),
            pltpu.VMEM((units, rows), jnp.bfloat16),
        ],
        compiler_params=pltpu.CompilerParams(vmem_limit_bytes=VMEM_LIMIT),
        cost_estimate=pl.CostEstimate(
            flops=12 * units * rows * owners * width, bytes_accessed=12 * 2**20, transcendentals=units * rows
        ),
        name="grads",
    )(w, xp, yp)


def input_partial(slot_of, core, w, dgu):
    owners, _, units, width = w.shape
    rows = dgu.shape[1]
    smem = pl.BlockSpec(memory_space=pltpu.SMEM)
    vmem = pl.BlockSpec(memory_space=pltpu.VMEM)
    shape = (owners, width // 2, rows)
    return pl.pallas_call(
        input_kernel,
        out_shape=(jax.ShapeDtypeStruct(shape, jnp.float32), jax.ShapeDtypeStruct(shape, jnp.bfloat16)),
        in_specs=[smem, smem, vmem, vmem],
        out_specs=(vmem, vmem),
        compiler_params=pltpu.CompilerParams(vmem_limit_bytes=VMEM_LIMIT),
        cost_estimate=pl.CostEstimate(flops=1000, bytes_accessed=1000, transcendentals=0),
        name="input_partial",
    )(slot_of, core, w, dgu)


def pair_sums(keep, came):
    tiles, feats, rows = keep.shape
    vmem = pl.BlockSpec(memory_space=pltpu.VMEM)
    part = (2, feats, rows)
    steps = tiles // 2
    return pl.pallas_call(
        pair_kernel,
        out_shape=(jax.ShapeDtypeStruct(part, jnp.float32),)
        + (jax.ShapeDtypeStruct(part, jnp.bfloat16),) * (steps - 1),
        in_specs=[vmem, vmem],
        out_specs=(vmem,) * steps,
        compiler_params=pltpu.CompilerParams(vmem_limit_bytes=VMEM_LIMIT),
        cost_estimate=pl.CostEstimate(flops=1000, bytes_accessed=1000, transcendentals=0),
        name="pair_sums",
    )(keep, came)


def update(modules_of, counts, delta, owned, momentum):
    paths = delta.shape[0]
    modules, mats, units, width = owned.shape
    rows = units // 2
    smem = pl.BlockSpec(memory_space=pltpu.SMEM)
    tile = pl.BlockSpec((modules, 1, rows, width), lambda k, i: (0, k, i, 0))
    return pl.pallas_call(
        update_kernel,
        grid=(mats, units // rows),
        out_shape=(jax.ShapeDtypeStruct(momentum.shape, jnp.float32),) * 2,
        in_specs=[
            smem,
            smem,
            pl.BlockSpec((paths, 1, rows, width), lambda k, i: (0, k, i, 0)),
            tile,
            tile,
        ],
        out_specs=(tile, tile),
        scratch_shapes=[pltpu.VMEM((modules, rows, width), jnp.float32)],
        compiler_params=pltpu.CompilerParams(vmem_limit_bytes=VMEM_LIMIT),
        cost_estimate=pl.CostEstimate(flops=10**6, bytes_accessed=8 * 2**20, transcendentals=0),
        name="update",
    )(modules_of, counts, delta, owned, momentum)


def pick(array, index):
    return array.at[index].get(mode="promise_in_bounds")


def turn(size, k):
    return [(i, (i + k) % size) for i in range(size)]


def ring_gather(piece, beside):
    depth = lax.axis_size("z")
    first = lax.axis_index("yl") == 0
    pair = jnp.concatenate([jnp.where(first, piece, beside), jnp.where(first, beside, piece)], axis=0)
    half = piece.shape[0]
    up = down = pair
    parts = [pair]
    at = [0] * depth
    for k in range(1, depth // 2):
        up = lax.ppermute(up, "z", turn(depth, 1))
        down = lax.ppermute(down, "z", turn(depth, -1))
        at[depth - k] = len(parts)
        at[k] = len(parts) + 1
        parts += [up, down]
    at[depth // 2] = len(parts)
    parts.append(lax.ppermute(up[:half], "z", turn(depth, 1)))
    parts.append(lax.ppermute(down[half:], "z", turn(depth, -1)))
    return jnp.concatenate(parts, axis=0), at


def body(tokens, cotangent, weights, momentum, cluster, path_module, owner):
    paths = lax.axis_size(PATH)
    here = lax.axis_index(PATH)
    core = lax.axis_index("c")
    modules_of = path_module[:, 0]
    path_ids = jnp.arange(paths, dtype=jnp.int32)
    blocks = tokens.shape[0] // BLK
    cols = tokens.shape[1]
    owned = weights[0]

    def feature_major(array):
        return array.reshape(blocks, BLK, cols).transpose(0, 2, 1)

    both = jnp.stack([feature_major(tokens), feature_major(cotangent)], axis=1)
    own_dest = lax.dynamic_slice_in_dim(cluster, here * blocks, blocks)
    goes = own_dest[None, :] == path_ids[:, None]
    block_ids = jnp.arange(blocks, dtype=jnp.int32)
    send_x = pick(both, jnp.sum(jnp.where(goes, block_ids[None, :], 0), axis=1))
    recv_x = lax.all_to_all(
        send_x.reshape(paths * 2, cols, BLK), PATH + ("c",), split_axis=0, concat_axis=0, tiled=True
    ).reshape(paths, 2, cols, BLK)
    has = jnp.any(cluster.reshape(paths, blocks) == here, axis=1)
    before = jnp.sum((has[None, :] & (path_ids[None, :] < path_ids[:, None])).astype(jnp.int32), axis=1)
    comes = has[None, :] & (before[None, :] == block_ids[:, None])
    sources = jnp.sum(jnp.where(comes, path_ids[None, :], 0), axis=1)
    piece = pick(recv_x, sources).transpose(1, 2, 0, 3).reshape(2 * cols, blocks * BLK)

    beside = lax.ppermute(piece, "yl", [(0, 1), (1, 0)])
    send_w, piece, beside = lax.optimization_barrier((pick(owned, modules_of), piece, beside))
    recv_w = lax.all_to_all(send_w, PATH, split_axis=0, concat_axis=0, tiled=True)
    mine, at = ring_gather(piece, beside)
    swap = [(0, 1), (1, 0)]
    other = lax.ppermute(mine, "c", swap)

    owner_row = owner[modules_of[here]]
    tile_of = jnp.sum(jnp.where(owner_row[None, :] == path_ids[:, None], path_ids[None, :], 0), axis=1)
    z = lax.axis_index("z")
    depth = lax.axis_size("z")
    away = (tile_of % depth - z) % depth
    side = tile_of // depth
    place = jnp.sum(jnp.where(away[:, None] == jnp.arange(depth)[None, :], jnp.array(at, jnp.int32)[None, :], 0), axis=1)
    core_id = core.reshape(1)
    xp, yp = in_owner_order(place * 2 + side, core_id, mine, other)
    delta, dgu = grads(recv_w, xp, yp)
    recv_delta = lax.all_to_all(delta, PATH, split_axis=0, concat_axis=0, tiled=True)

    keep, give = input_partial(away * 2 + side, core_id, recv_w, dgu)
    sums = pair_sums(keep, lax.ppermute(give, "c", swap))
    came = [lax.ppermute(sums[k], "z", turn(depth, k)) for k in range(1, depth)]
    total = sums[0]
    for part in came:
        total = total + part.astype(jnp.float32)
    yl = lax.axis_index("yl")
    total, recv_delta = lax.optimization_barrier((total, recv_delta))
    theirs = lax.ppermute(lax.dynamic_index_in_dim(total, 1 - yl, 0, keepdims=False), "yl", swap)
    total = lax.dynamic_index_in_dim(total, yl, 0, keepdims=False) + theirs
    input_grad = total.astype(jnp.bfloat16).T

    member = modules_of[None, :] == jnp.arange(MODULES, dtype=jnp.int32)[:, None]
    counts = jnp.sum(member.astype(jnp.float32), axis=1)
    new_tiles, new_moment = update(modules_of, counts, recv_delta, owned, momentum[0])
    return (input_grad, new_tiles[None], new_moment[None])


def solution(mesh):
    fine = Mesh(mesh.devices.reshape(4, 4, 2, 8, 2), PATH + SHARD)
    tiles = P(PATH, None, None, SHARD, None)
    return jax.shard_map(
        body,
        mesh=fine,
        in_specs=(P(PATH, SHARD), P(PATH, SHARD), tiles, tiles, P(), P(), P()),
        out_specs=(P(PATH, SHARD), tiles, tiles),
        check_vma=False,
    )
```

```python
import jax
import jax.numpy as jnp
from jax import lax
from jax.experimental import pallas as pl
from jax.experimental.pallas import tpu as pltpu
from jax.sharding import Mesh, PartitionSpec as P

MODULES = 4
BLK = 128
MU = 0.9
LR_INNER = 0.05
LR_OUTER = 0.02

PATH = ("yh", "x")
SHARD = ("yl", "z", "c")
BIG = ("x", "yh")
VMEM_LIMIT = 24 * 1024 * 1024


def pack_kernel(cluster_ref, here_ref, tokens_hbm, cotangent_hbm, send_ref, tokens_ref, cotangent_ref, sem):
    load_t = pltpu.make_async_copy(tokens_hbm, tokens_ref, sem.at[0])
    load_c = pltpu.make_async_copy(cotangent_hbm, cotangent_ref, sem.at[1])
    load_t.start()
    load_c.start()
    load_t.wait()
    load_c.wait()
    blocks = tokens_ref.shape[1] // BLK

    def block(b):
        lanes = slice(b * BLK, (b + 1) * BLK)
        return jnp.stack([tokens_ref[:, lanes], cotangent_ref[:, lanes]])

    def fill(d, carry):
        send_ref[d] = block(0)
        return carry

    lax.fori_loop(0, send_ref.shape[0], fill, 0)
    for b in range(blocks):
        send_ref[cluster_ref[here_ref[0] * blocks + b]] = block(b)


def grads_kernel(
    place_ref, core_ref, w_ref, mine_hbm, other_hbm, delta_hbm, dgu_hbm, xp, yp, delta, dgu, g_s, u_s, d_s, h_s, in_sem, out_sem
):
    owners, _, units, width = w_ref.shape

    def fetch(source, target, base):
        for o in range(owners):
            here = pl.ds(pl.multiple_of(place_ref[o] * width, width), width)
            pltpu.make_async_copy(source.at[here], target.at[pl.ds(o * width, width)], in_sem.at[base + o]).start()

    @pl.when(core_ref[0] == 0)
    def _():
        fetch(mine_hbm, xp, 0)
        fetch(other_hbm, yp, owners)

    @pl.when(core_ref[0] != 0)
    def _():
        fetch(other_hbm, xp, 0)
        fetch(mine_hbm, yp, owners)

    def arrived(target, base, some):
        for o in some:
            rows = pl.ds(o * width, width)
            pltpu.make_async_copy(mine_hbm.at[rows], target.at[rows], in_sem.at[base + o]).wait()

    def product(k, tokens, some):
        left = jnp.concatenate([w_ref[o, k] for o in some], axis=1)
        right = tokens[some[0] * width : (some[-1] + 1) * width, :]
        return jnp.dot(left, right, preferred_element_type=jnp.float32)

    early, late = range(owners // 2), range(owners // 2, owners)
    arrived(xp, 0, early)
    g_s[...] = product(0, xp, early)
    u_s[...] = product(1, xp, early)
    arrived(xp, 0, late)
    g_s[...] += product(0, xp, late)
    u_s[...] += product(1, xp, late)
    arrived(yp, owners, range(owners))
    d_s[...] = product(2, yp, range(owners))
    step = 32

    def act(i, carry):
        at = pl.multiple_of(i * step, step)
        rows = pl.ds(at, step)
        gate = g_s[rows, :]
        up = u_s[rows, :]
        dh = d_s[rows, :]
        sig = jax.nn.sigmoid(gate)
        silu = gate * sig
        h_s[rows, :] = (silu * up).astype(jnp.bfloat16)
        dgu[rows, :] = (dh * up * sig * (1.0 + gate * (1.0 - sig))).astype(jnp.bfloat16)
        dgu[pl.ds(pl.multiple_of(units + at, step), step), :] = (dh * silu).astype(jnp.bfloat16)
        return carry

    lax.fori_loop(0, units // step, act, 0)
    save_dgu = pltpu.make_async_copy(dgu, dgu_hbm, out_sem.at[owners // 2])
    save_dgu.start()
    nt = (((1,), (1,)), ((), ()))
    saves = []
    for p in range(owners // 2):
        rows = slice(p * 2 * width, (p + 1) * 2 * width)
        gu = LR_INNER * lax.dot_general(dgu[...], xp[rows, :], nt, preferred_element_type=jnp.float32)
        dn = LR_INNER * lax.dot_general(h_s[...], yp[rows, :], nt, preferred_element_type=jnp.float32)
        gu = gu.astype(jnp.bfloat16)
        dn = dn.astype(jnp.bfloat16)
        for half in range(2):
            lanes = slice(half * width, (half + 1) * width)
            delta[2 * p + half, 0] = gu[:units, lanes]
            delta[2 * p + half, 1] = gu[units:, lanes]
            delta[2 * p + half, 2] = dn[:, lanes]
        pair = slice(2 * p, 2 * p + 2)
        save = pltpu.make_async_copy(delta.at[pair], delta_hbm.at[pair], out_sem.at[p])
        save.start()
        saves.append(save)
    for save in saves:
        save.wait()
    save_dgu.wait()


def input_kernel(slot_ref, core_ref, w_ref, dgu_ref, keep_ref, give_ref):
    owners, _, units, width = w_ref.shape
    half = width // 2
    core = core_ref[0]

    def one(o, carry):
        w = w_ref[o, 0:2].reshape(2 * units, width)
        part = lax.dot_general(w, dgu_ref[...], (((0,), (0,)), ((), ())), preferred_element_type=jnp.float32)
        j = slot_ref[o]
        low, high = part[:half], part[half:]
        keep_ref[j] = jnp.where(core == 0, low, high)
        give_ref[j] = jnp.where(core == 0, high, low).astype(jnp.bfloat16)
        return carry

    lax.fori_loop(0, owners, one, 0)


def pair_kernel(keep_ref, came_ref, own_ref, *out_refs):
    for k in range(len(out_refs) + 1):
        at = slice(2 * k, 2 * k + 2)
        total = keep_ref[at] + came_ref[at].astype(jnp.float32)
        if k == 0:
            own_ref[...] = total
        else:
            out_refs[k - 1][...] = total.astype(jnp.bfloat16)


def update_kernel(module_ref, scale_ref, delta_ref, w_ref, m_ref, new_w_hbm, new_m_hbm, new_w, new_m, acc, out_sem):
    modules, mats, units, width = w_ref.shape
    paths = delta_ref.shape[0]
    step = acc.shape[1]
    saves = []
    for k in range(mats):
        for i in range(units // step):
            rows = slice(i * step, (i + 1) * step)
            acc[...] = jnp.zeros_like(acc)
            for q in range(paths):
                acc[module_ref[q]] += delta_ref[q, k, rows, :].astype(jnp.float32)
            for m in range(modules):
                mean = acc[m] * scale_ref[m]
                moment = MU * m_ref[m, k, rows, :] + mean
                new_m[m, k, rows, :] = moment
                new_w[m, k, rows, :] = w_ref[m, k, rows, :].astype(jnp.float32) - LR_OUTER * (mean + MU * moment)
            for here, there in ((new_w, new_w_hbm), (new_m, new_m_hbm)):
                part = (slice(None), k, rows)
                save = pltpu.make_async_copy(here.at[part], there.at[part], out_sem.at[len(saves)])
                save.start()
                saves.append(save)
    for save in saves:
        save.wait()


def in_hbm(array):
    return pltpu.with_memory_space_constraint(array, pltpu.HBM)


def pack(cluster, here, tokens, cotangent):
    cols, rows = tokens.shape
    paths = cluster.shape[0] * BLK // rows
    smem = pl.BlockSpec(memory_space=pltpu.SMEM)
    vmem = pl.BlockSpec(memory_space=pltpu.VMEM)
    hbm = pl.BlockSpec(memory_space=pltpu.HBM)
    return pl.pallas_call(
        pack_kernel,
        out_shape=jax.ShapeDtypeStruct((paths, 2, cols, BLK), tokens.dtype),
        in_specs=[smem, smem, hbm, hbm],
        out_specs=vmem,
        scratch_shapes=[pltpu.VMEM(tokens.shape, tokens.dtype)] * 2 + [pltpu.SemaphoreType.DMA((2,))],
        compiler_params=pltpu.CompilerParams(vmem_limit_bytes=VMEM_LIMIT),
        cost_estimate=pl.CostEstimate(flops=1000, bytes_accessed=1000, transcendentals=0),
        name="pack",
    )(cluster, here, in_hbm(tokens), in_hbm(cotangent))


def grads(place, core, w, mine, other):
    owners, _, units, width = w.shape
    rows = mine.shape[1]
    smem = pl.BlockSpec(memory_space=pltpu.SMEM)
    vmem = pl.BlockSpec(memory_space=pltpu.VMEM)
    hbm = pl.BlockSpec(memory_space=pltpu.HBM)
    return pl.pallas_call(
        grads_kernel,
        out_shape=(
            pltpu.HBM(w.shape, jnp.bfloat16),
            pltpu.HBM((2 * units, rows), jnp.bfloat16),
        ),
        in_specs=[smem, smem, vmem, hbm, hbm],
        out_specs=(hbm, hbm),
        scratch_shapes=[
            pltpu.VMEM(mine.shape, jnp.bfloat16),
            pltpu.VMEM(mine.shape, jnp.bfloat16),
            pltpu.VMEM(w.shape, jnp.bfloat16),
            pltpu.VMEM((2 * units, rows), jnp.bfloat16),
            pltpu.VMEM((units, rows), jnp.float32),
            pltpu.VMEM((units, rows), jnp.float32),
            pltpu.VMEM((units, rows), jnp.float32),
            pltpu.VMEM((units, rows), jnp.bfloat16),
            pltpu.SemaphoreType.DMA((2 * owners,)),
            pltpu.SemaphoreType.DMA((owners // 2 + 1,)),
        ],
        compiler_params=pltpu.CompilerParams(vmem_limit_bytes=VMEM_LIMIT),
        cost_estimate=pl.CostEstimate(
            flops=12 * units * rows * owners * width, bytes_accessed=12 * 2**20, transcendentals=units * rows
        ),
        name="grads",
    )(place, core, w, in_hbm(mine), in_hbm(other))


def input_partial(slot_of, core, w, dgu):
    owners, _, units, width = w.shape
    rows = dgu.shape[1]
    smem = pl.BlockSpec(memory_space=pltpu.SMEM)
    vmem = pl.BlockSpec(memory_space=pltpu.VMEM)
    shape = (owners, width // 2, rows)
    return pl.pallas_call(
        input_kernel,
        out_shape=(jax.ShapeDtypeStruct(shape, jnp.float32), jax.ShapeDtypeStruct(shape, jnp.bfloat16)),
        in_specs=[smem, smem, vmem, vmem],
        out_specs=(vmem, vmem),
        compiler_params=pltpu.CompilerParams(vmem_limit_bytes=VMEM_LIMIT),
        cost_estimate=pl.CostEstimate(flops=1000, bytes_accessed=1000, transcendentals=0),
        name="input_partial",
    )(slot_of, core, w, dgu)


def pair_sums(keep, came):
    tiles, feats, rows = keep.shape
    vmem = pl.BlockSpec(memory_space=pltpu.VMEM)
    part = (2, feats, rows)
    steps = tiles // 2
    return pl.pallas_call(
        pair_kernel,
        out_shape=(jax.ShapeDtypeStruct(part, jnp.float32),)
        + (jax.ShapeDtypeStruct(part, jnp.bfloat16),) * (steps - 1),
        in_specs=[vmem, vmem],
        out_specs=(vmem,) * steps,
        compiler_params=pltpu.CompilerParams(vmem_limit_bytes=VMEM_LIMIT),
        cost_estimate=pl.CostEstimate(flops=1000, bytes_accessed=1000, transcendentals=0),
        name="pair_sums",
    )(keep, came)


def update(modules_of, scale, delta, owned, momentum):
    modules, mats, units, width = owned.shape
    smem = pl.BlockSpec(memory_space=pltpu.SMEM)
    vmem = pl.BlockSpec(memory_space=pltpu.VMEM)
    hbm = pl.BlockSpec(memory_space=pltpu.HBM)
    return pl.pallas_call(
        update_kernel,
        out_shape=(jax.ShapeDtypeStruct(momentum.shape, jnp.float32),) * 2,
        in_specs=[smem, smem, vmem, vmem, vmem],
        out_specs=(hbm, hbm),
        scratch_shapes=[
            pltpu.VMEM(momentum.shape, jnp.float32),
            pltpu.VMEM(momentum.shape, jnp.float32),
            pltpu.VMEM((modules, units // 2, width), jnp.float32),
            pltpu.SemaphoreType.DMA((4 * mats,)),
        ],
        compiler_params=pltpu.CompilerParams(vmem_limit_bytes=VMEM_LIMIT // 2),
        cost_estimate=pl.CostEstimate(flops=10**6, bytes_accessed=8 * 2**20, transcendentals=0),
        name="update",
    )(modules_of, scale, delta, owned, momentum)


def pick(array, index):
    return array.at[index].get(mode="promise_in_bounds")


def transposed(per_path):
    lead = per_path.shape[:-1]
    grid = per_path.reshape(lead + tuple(lax.axis_size(name) for name in PATH))
    return jnp.swapaxes(grid, -1, -2).reshape(per_path.shape)


def turn(size, k):
    return [(i, (i + k) % size) for i in range(size)]


def ring_gather(piece, beside):
    depth = lax.axis_size("z")
    first = lax.axis_index("yl") == 0
    pair = jnp.concatenate([jnp.where(first, piece, beside), jnp.where(first, beside, piece)], axis=0)
    half = piece.shape[0]
    up = down = pair
    parts = [pair]
    at = [0] * depth
    for k in range(1, depth // 2):
        up = lax.ppermute(up, "z", turn(depth, 1))
        down = lax.ppermute(down, "z", turn(depth, -1))
        at[depth - k] = len(parts)
        at[k] = len(parts) + 1
        parts += [up, down]
    at[depth // 2] = len(parts)
    parts.append(lax.ppermute(up[:half], "z", turn(depth, 1)))
    parts.append(lax.ppermute(down[half:], "z", turn(depth, -1)))
    return jnp.concatenate(parts, axis=0), at


def body(tokens, cotangent, weights, momentum, cluster, path_module, owner):
    paths = lax.axis_size(PATH)
    here = lax.axis_index(PATH)
    core = lax.axis_index("c")
    modules_of = path_module[:, 0]
    path_ids = jnp.arange(paths, dtype=jnp.int32)
    blocks = tokens.shape[0] // BLK
    cols = tokens.shape[1]
    owned = weights[0]

    block_ids = jnp.arange(blocks, dtype=jnp.int32)
    send_x = pack(cluster, here.reshape(1), tokens.T, cotangent.T)
    recv_x = lax.all_to_all(
        send_x.reshape(paths * 2, cols, BLK), PATH + ("c",), split_axis=0, concat_axis=0, tiled=True
    ).reshape(paths, 2, cols, BLK)
    has = jnp.any(cluster.reshape(paths, blocks) == here, axis=1)
    before = jnp.sum((has[None, :] & (path_ids[None, :] < path_ids[:, None])).astype(jnp.int32), axis=1)
    comes = has[None, :] & (before[None, :] == block_ids[:, None])
    sources = jnp.sum(jnp.where(comes, path_ids[None, :], 0), axis=1)
    piece = pick(recv_x, sources).transpose(1, 2, 0, 3).reshape(2 * cols, blocks * BLK)

    beside = lax.ppermute(piece, "yl", [(0, 1), (1, 0)])
    send_w, piece, beside = lax.optimization_barrier((pick(owned, transposed(modules_of)), piece, beside))
    recv_w = lax.all_to_all(send_w, BIG, split_axis=0, concat_axis=0, tiled=True)
    mine, at = ring_gather(piece, beside)
    swap = [(0, 1), (1, 0)]
    other = lax.ppermute(mine, "c", swap)

    owner_row = owner[modules_of[here]]
    tile_of = jnp.sum(jnp.where(owner_row[None, :] == transposed(path_ids)[:, None], path_ids[None, :], 0), axis=1)
    z = lax.axis_index("z")
    depth = lax.axis_size("z")
    away = (tile_of % depth - z) % depth
    side = tile_of // depth
    place = jnp.sum(jnp.where(away[:, None] == jnp.arange(depth)[None, :], jnp.array(at, jnp.int32)[None, :], 0), axis=1)
    core_id = core.reshape(1)
    delta, dgu = grads(place * 2 + side, core_id, recv_w, mine, other)
    recv_delta = lax.all_to_all(delta, BIG, split_axis=0, concat_axis=0, tiled=True)

    keep, give = input_partial(away * 2 + side, core_id, recv_w, dgu)
    sums = pair_sums(keep, lax.ppermute(give, "c", swap))
    came = [lax.ppermute(sums[k], "z", turn(depth, k)) for k in range(1, depth)]
    total = sums[0]
    for part in came:
        total = total + part.astype(jnp.float32)
    yl = lax.axis_index("yl")
    theirs = lax.ppermute(lax.dynamic_index_in_dim(total, 1 - yl, 0, keepdims=False), "yl", swap)
    member = modules_of[None, :] == jnp.arange(MODULES, dtype=jnp.int32)[:, None]
    counts = jnp.sum(member.astype(jnp.float32), axis=1)
    new_tiles, new_moment = update(transposed(modules_of), 1.0 / counts, recv_delta, owned, momentum[0])
    total, new_moment = lax.optimization_barrier((lax.dynamic_index_in_dim(total, yl, 0, keepdims=False), new_moment))
    input_grad = (total + theirs).astype(jnp.bfloat16).T
    return (input_grad, new_tiles[None], new_moment[None])


def solution(mesh):
    fine = Mesh(mesh.devices.reshape(4, 4, 2, 8, 2), PATH + SHARD)
    tiles = P(PATH, None, None, SHARD, None)
    return jax.shard_map(
        body,
        mesh=fine,
        in_specs=(P(PATH, SHARD), P(PATH, SHARD), tiles, tiles, P(), P(), P()),
        out_specs=(P(PATH, SHARD), tiles, tiles),
        check_vma=False,
    )
```

```python
import jax
import jax.numpy as jnp
from jax import lax
from jax.experimental import pallas as pl
from jax.experimental.pallas import tpu as pltpu
from jax.sharding import Mesh, PartitionSpec as P

MODULES = 4
BLK = 128
MU = 0.9
LR_INNER = 0.05
LR_OUTER = 0.02

PATH = ("yh", "x")
SHARD = ("yl", "z", "c")
BIG = ("x", "yh")
VMEM_LIMIT = 24 * 1024 * 1024


def pack_kernel(here_ref, cluster_hbm, tokens_hbm, cotangent_hbm, send_hbm, cluster_ref, tokens_ref, cotangent_ref, in_sem, out_sem):
    blocks = tokens_ref.shape[1] // BLK
    pairs = ((cluster_hbm, cluster_ref), (tokens_hbm, tokens_ref), (cotangent_hbm, cotangent_ref))
    loads = [pltpu.make_async_copy(there, here, in_sem.at[i]) for i, (there, here) in enumerate(pairs)]
    for load in loads:
        load.start()
    for load in loads:
        load.wait()
    saves = []
    for b in range(blocks):
        to = cluster_ref[here_ref[0] * blocks + b]
        for i, source in enumerate((tokens_ref, cotangent_ref)):
            lanes = source.at[:, pl.ds(b * BLK, BLK)]
            saves.append(pltpu.make_async_copy(lanes, send_hbm.at[to, i], out_sem.at[2 * b + i]))
            saves[-1].start()
    for save in saves:
        save.wait()


def grads_kernel(
    place_ref, core_ref, w_ref, mine_hbm, other_hbm, delta_hbm, dgu_hbm, xp, yp, delta, dgu, g_s, u_s, d_s, h_s, in_sem, out_sem
):
    owners, _, units, width = w_ref.shape

    def fetch(source, target, base):
        for o in range(owners):
            here = pl.ds(pl.multiple_of(place_ref[o] * width, width), width)
            pltpu.make_async_copy(source.at[here], target.at[pl.ds(o * width, width)], in_sem.at[base + o]).start()

    @pl.when(core_ref[0] == 0)
    def _():
        fetch(mine_hbm, xp, 0)
        fetch(other_hbm, yp, owners)

    @pl.when(core_ref[0] != 0)
    def _():
        fetch(other_hbm, xp, 0)
        fetch(mine_hbm, yp, owners)

    def arrived(target, base, some):
        for o in some:
            rows = pl.ds(o * width, width)
            pltpu.make_async_copy(mine_hbm.at[rows], target.at[rows], in_sem.at[base + o]).wait()

    def product(k, tokens, some):
        left = jnp.concatenate([w_ref[o, k] for o in some], axis=1)
        right = tokens[some[0] * width : (some[-1] + 1) * width, :]
        return jnp.dot(left, right, preferred_element_type=jnp.float32)

    early, late = range(owners // 2), range(owners // 2, owners)
    arrived(xp, 0, early)
    g_s[...] = product(0, xp, early)
    u_s[...] = product(1, xp, early)
    arrived(xp, 0, late)
    g_s[...] += product(0, xp, late)
    u_s[...] += product(1, xp, late)
    arrived(yp, owners, early)
    d_s[...] = product(2, yp, early)
    arrived(yp, owners, late)
    d_s[...] += product(2, yp, late)
    step = 32

    def act(i, carry):
        at = pl.multiple_of(i * step, step)
        rows = pl.ds(at, step)
        gate = g_s[rows, :]
        up = u_s[rows, :]
        dh = d_s[rows, :]
        sig = jax.nn.sigmoid(gate)
        silu = gate * sig
        h_s[rows, :] = (silu * up).astype(jnp.bfloat16)
        dgu[rows, :] = (dh * up * sig * (1.0 + gate * (1.0 - sig))).astype(jnp.bfloat16)
        dgu[pl.ds(pl.multiple_of(units + at, step), step), :] = (dh * silu).astype(jnp.bfloat16)
        return carry

    lax.fori_loop(0, units // step, act, 0)
    save_dgu = pltpu.make_async_copy(dgu, dgu_hbm, out_sem.at[owners // 2])
    save_dgu.start()
    nt = (((1,), (1,)), ((), ()))
    saves = []
    for p in range(owners // 2):
        rows = slice(p * 2 * width, (p + 1) * 2 * width)
        gu = LR_INNER * lax.dot_general(dgu[...], xp[rows, :], nt, preferred_element_type=jnp.float32)
        dn = LR_INNER * lax.dot_general(h_s[...], yp[rows, :], nt, preferred_element_type=jnp.float32)
        gu = gu.astype(jnp.bfloat16)
        dn = dn.astype(jnp.bfloat16)
        for half in range(2):
            lanes = slice(half * width, (half + 1) * width)
            delta[2 * p + half, 0] = gu[:units, lanes]
            delta[2 * p + half, 1] = gu[units:, lanes]
            delta[2 * p + half, 2] = dn[:, lanes]
        pair = slice(2 * p, 2 * p + 2)
        save = pltpu.make_async_copy(delta.at[pair], delta_hbm.at[pair], out_sem.at[p])
        save.start()
        saves.append(save)
    for save in saves:
        save.wait()
    save_dgu.wait()


def input_kernel(slot_ref, core_ref, w_ref, dgu_ref, keep_ref, give_ref):
    owners, _, units, width = w_ref.shape
    half = width // 2
    core = core_ref[0]

    for o in range(owners):
        w = w_ref[o, 0:2].reshape(2 * units, width)
        part = lax.dot_general(w, dgu_ref[...], (((0,), (0,)), ((), ())), preferred_element_type=jnp.float32)
        j = slot_ref[o]
        low, high = part[:half], part[half:]
        keep_ref[j] = jnp.where(core == 0, low, high)
        give_ref[j] = jnp.where(core == 0, high, low).astype(jnp.bfloat16)


def pair_kernel(keep_ref, came_ref, own_ref, *out_refs):
    for k in range(len(out_refs) + 1):
        at = slice(2 * k, 2 * k + 2)
        total = keep_ref[at] + came_ref[at].astype(jnp.float32)
        if k == 0:
            own_ref[...] = total
        else:
            out_refs[k - 1][...] = total.astype(jnp.bfloat16)


def update_kernel(
    module_ref, scale_ref, delta_hbm, w_ref, m_ref, new_w_hbm, new_m_hbm, delta_ref, new_w, new_m, acc, in_sem, out_sem
):
    modules, mats, units, width = w_ref.shape
    paths = delta_ref.shape[0]
    step = acc.shape[1]
    parts = [(k, slice(i * step, (i + 1) * step)) for k in range(mats) for i in range(units // step)]
    loads = []
    for k, rows in parts:
        part = (slice(None), k, rows)
        loads.append(pltpu.make_async_copy(delta_hbm.at[part], delta_ref.at[part], in_sem.at[len(loads)]))
        loads[-1].start()
    saves = []
    for load, (k, rows) in zip(loads, parts):
        load.wait()
        acc[...] = jnp.zeros_like(acc)
        for q in range(paths):
            acc[module_ref[q]] += delta_ref[q, k, rows, :].astype(jnp.float32)
        for m in range(modules):
            mean = acc[m] * scale_ref[m]
            moment = MU * m_ref[m, k, rows, :] + mean
            new_m[m, k, rows, :] = moment
            new_w[m, k, rows, :] = w_ref[m, k, rows, :].astype(jnp.float32) - LR_OUTER * (mean + MU * moment)
        for here, there in ((new_w, new_w_hbm), (new_m, new_m_hbm)):
            part = (slice(None), k, rows)
            save = pltpu.make_async_copy(here.at[part], there.at[part], out_sem.at[len(saves)])
            save.start()
            saves.append(save)
    for save in saves:
        save.wait()


def in_hbm(array):
    return pltpu.with_memory_space_constraint(array, pltpu.HBM)


def pack(here, cluster, tokens, cotangent):
    cols, rows = tokens.shape
    blocks = rows // BLK
    paths = cluster.shape[0] // blocks
    smem = pl.BlockSpec(memory_space=pltpu.SMEM)
    hbm = pl.BlockSpec(memory_space=pltpu.HBM)
    return pl.pallas_call(
        pack_kernel,
        out_shape=pltpu.HBM((paths, 2, cols, BLK), tokens.dtype),
        in_specs=[smem, hbm, hbm, hbm],
        out_specs=hbm,
        scratch_shapes=[
            pltpu.SMEM(cluster.shape, cluster.dtype),
            pltpu.VMEM(tokens.shape, tokens.dtype),
            pltpu.VMEM(tokens.shape, tokens.dtype),
            pltpu.SemaphoreType.DMA((3,)),
            pltpu.SemaphoreType.DMA((2 * blocks,)),
        ],
        compiler_params=pltpu.CompilerParams(vmem_limit_bytes=VMEM_LIMIT),
        cost_estimate=pl.CostEstimate(flops=1000, bytes_accessed=1000, transcendentals=0),
        name="pack",
    )(here, in_hbm(cluster), in_hbm(tokens), in_hbm(cotangent))


def grads(place, core, w, mine, other):
    owners, _, units, width = w.shape
    rows = mine.shape[1]
    smem = pl.BlockSpec(memory_space=pltpu.SMEM)
    vmem = pl.BlockSpec(memory_space=pltpu.VMEM)
    hbm = pl.BlockSpec(memory_space=pltpu.HBM)
    return pl.pallas_call(
        grads_kernel,
        out_shape=(
            pltpu.HBM(w.shape, jnp.bfloat16),
            pltpu.HBM((2 * units, rows), jnp.bfloat16),
        ),
        in_specs=[smem, smem, vmem, hbm, hbm],
        out_specs=(hbm, hbm),
        scratch_shapes=[
            pltpu.VMEM(mine.shape, jnp.bfloat16),
            pltpu.VMEM(mine.shape, jnp.bfloat16),
            pltpu.VMEM(w.shape, jnp.bfloat16),
            pltpu.VMEM((2 * units, rows), jnp.bfloat16),
            pltpu.VMEM((units, rows), jnp.float32),
            pltpu.VMEM((units, rows), jnp.float32),
            pltpu.VMEM((units, rows), jnp.float32),
            pltpu.VMEM((units, rows), jnp.bfloat16),
            pltpu.SemaphoreType.DMA((2 * owners,)),
            pltpu.SemaphoreType.DMA((owners // 2 + 1,)),
        ],
        compiler_params=pltpu.CompilerParams(vmem_limit_bytes=VMEM_LIMIT),
        cost_estimate=pl.CostEstimate(
            flops=12 * units * rows * owners * width, bytes_accessed=12 * 2**20, transcendentals=units * rows
        ),
        name="grads",
    )(place, core, w, in_hbm(mine), in_hbm(other))


def input_partial(slot_of, core, w, dgu):
    owners, _, units, width = w.shape
    rows = dgu.shape[1]
    smem = pl.BlockSpec(memory_space=pltpu.SMEM)
    vmem = pl.BlockSpec(memory_space=pltpu.VMEM)
    shape = (owners, width // 2, rows)
    return pl.pallas_call(
        input_kernel,
        out_shape=(jax.ShapeDtypeStruct(shape, jnp.float32), jax.ShapeDtypeStruct(shape, jnp.bfloat16)),
        in_specs=[smem, smem, vmem, vmem],
        out_specs=(vmem, vmem),
        compiler_params=pltpu.CompilerParams(vmem_limit_bytes=VMEM_LIMIT),
        cost_estimate=pl.CostEstimate(flops=1000, bytes_accessed=1000, transcendentals=0),
        name="input_partial",
    )(slot_of, core, w, dgu)


def pair_sums(keep, came):
    tiles, feats, rows = keep.shape
    vmem = pl.BlockSpec(memory_space=pltpu.VMEM)
    part = (2, feats, rows)
    steps = tiles // 2
    return pl.pallas_call(
        pair_kernel,
        out_shape=(jax.ShapeDtypeStruct(part, jnp.float32),)
        + (jax.ShapeDtypeStruct(part, jnp.bfloat16),) * (steps - 1),
        in_specs=[vmem, vmem],
        out_specs=(vmem,) * steps,
        compiler_params=pltpu.CompilerParams(vmem_limit_bytes=VMEM_LIMIT),
        cost_estimate=pl.CostEstimate(flops=1000, bytes_accessed=1000, transcendentals=0),
        name="pair_sums",
    )(keep, came)


def update(modules_of, scale, delta, owned, momentum):
    modules, mats, units, width = owned.shape
    smem = pl.BlockSpec(memory_space=pltpu.SMEM)
    vmem = pl.BlockSpec(memory_space=pltpu.VMEM)
    hbm = pl.BlockSpec(memory_space=pltpu.HBM)
    return pl.pallas_call(
        update_kernel,
        out_shape=(jax.ShapeDtypeStruct(momentum.shape, jnp.float32),) * 2,
        in_specs=[smem, smem, hbm, vmem, vmem],
        out_specs=(hbm, hbm),
        scratch_shapes=[
            pltpu.VMEM(delta.shape, delta.dtype),
            pltpu.VMEM(momentum.shape, jnp.float32),
            pltpu.VMEM(momentum.shape, jnp.float32),
            pltpu.VMEM((modules, units // 2, width), jnp.float32),
            pltpu.SemaphoreType.DMA((2 * mats,)),
            pltpu.SemaphoreType.DMA((4 * mats,)),
        ],
        compiler_params=pltpu.CompilerParams(vmem_limit_bytes=VMEM_LIMIT // 2),
        cost_estimate=pl.CostEstimate(flops=10**6, bytes_accessed=8 * 2**20, transcendentals=0),
        name="update",
    )(modules_of, scale, in_hbm(delta), owned, momentum)


def pick(array, index):
    return array.at[index].get(mode="promise_in_bounds")


def transposed(per_path):
    lead = per_path.shape[:-1]
    grid = per_path.reshape(lead + tuple(lax.axis_size(name) for name in PATH))
    return jnp.swapaxes(grid, -1, -2).reshape(per_path.shape)


def turn(size, k):
    return [(i, (i + k) % size) for i in range(size)]


def ring_gather(piece, beside):
    depth = lax.axis_size("z")
    first = lax.axis_index("yl") == 0
    pair = jnp.concatenate([jnp.where(first, piece, beside), jnp.where(first, beside, piece)], axis=0)
    half = piece.shape[0]
    up = down = pair
    parts = [pair]
    at = [0] * depth
    for k in range(1, depth // 2):
        up = lax.ppermute(up, "z", turn(depth, 1))
        down = lax.ppermute(down, "z", turn(depth, -1))
        at[depth - k] = len(parts)
        at[k] = len(parts) + 1
        parts += [up, down]
    at[depth // 2] = len(parts)
    parts.append(lax.ppermute(up[:half], "z", turn(depth, 1)))
    parts.append(lax.ppermute(down[half:], "z", turn(depth, -1)))
    return jnp.concatenate(parts, axis=0), at


def body(tokens, cotangent, weights, momentum, cluster, path_module, owner):
    paths = lax.axis_size(PATH)
    here = lax.axis_index(PATH)
    core = lax.axis_index("c")
    modules_of = path_module[:, 0]
    path_ids = jnp.arange(paths, dtype=jnp.int32)
    blocks = tokens.shape[0] // BLK
    cols = tokens.shape[1]
    owned = weights[0]

    block_ids = jnp.arange(blocks, dtype=jnp.int32)
    send_x = pack(here.reshape(1), cluster, tokens.T, cotangent.T)
    recv_x = lax.all_to_all(
        send_x.reshape(paths * 2, cols, BLK), PATH + ("c",), split_axis=0, concat_axis=0, tiled=True
    ).reshape(paths, 2, cols, BLK)
    has = jnp.any(cluster.reshape(paths, blocks) == here, axis=1)
    before = jnp.sum((has[None, :] & (path_ids[None, :] < path_ids[:, None])).astype(jnp.int32), axis=1)
    comes = has[None, :] & (before[None, :] == block_ids[:, None])
    sources = jnp.sum(jnp.where(comes, path_ids[None, :], 0), axis=1)
    piece = pick(recv_x, sources).transpose(1, 2, 0, 3).reshape(2 * cols, blocks * BLK)

    beside = lax.ppermute(piece, "yl", [(0, 1), (1, 0)])
    send_w, piece, beside = lax.optimization_barrier((pick(owned, transposed(modules_of)), piece, beside))
    recv_w = lax.all_to_all(send_w, BIG, split_axis=0, concat_axis=0, tiled=True)
    mine, at = ring_gather(piece, beside)
    swap = [(0, 1), (1, 0)]
    other = lax.ppermute(mine, "c", swap)

    owner_row = owner[modules_of[here]]
    tile_of = jnp.sum(jnp.where(owner_row[None, :] == transposed(path_ids)[:, None], path_ids[None, :], 0), axis=1)
    z = lax.axis_index("z")
    depth = lax.axis_size("z")
    away = (tile_of % depth - z) % depth
    side = tile_of // depth
    place = jnp.sum(jnp.where(away[:, None] == jnp.arange(depth)[None, :], jnp.array(at, jnp.int32)[None, :], 0), axis=1)
    core_id = core.reshape(1)
    delta, dgu = grads(place * 2 + side, core_id, recv_w, mine, other)
    recv_delta = lax.all_to_all(delta, BIG, split_axis=0, concat_axis=0, tiled=True)

    keep, give = input_partial(away * 2 + side, core_id, recv_w, dgu)
    sums = pair_sums(keep, lax.ppermute(give, "c", swap))
    came = [lax.ppermute(sums[k], "z", turn(depth, k)) for k in range(1, depth)]
    total = sums[0]
    for part in came:
        total = total + part.astype(jnp.float32)
    yl = lax.axis_index("yl")
    theirs = lax.ppermute(lax.dynamic_index_in_dim(total, 1 - yl, 0, keepdims=False), "yl", swap)
    member = modules_of[None, :] == jnp.arange(MODULES, dtype=jnp.int32)[:, None]
    counts = jnp.sum(member.astype(jnp.float32), axis=1)
    new_tiles, new_moment = update(transposed(modules_of), 1.0 / counts, recv_delta, owned, momentum[0])
    total, new_moment = lax.optimization_barrier((lax.dynamic_index_in_dim(total, yl, 0, keepdims=False), new_moment))
    input_grad = (total + theirs).astype(jnp.bfloat16).T
    return (input_grad, new_tiles[None], new_moment[None])


def solution(mesh):
    fine = Mesh(mesh.devices.reshape(4, 4, 2, 8, 2), PATH + SHARD)
    tiles = P(PATH, None, None, SHARD, None)
    return jax.shard_map(
        body,
        mesh=fine,
        in_specs=(P(PATH, SHARD), P(PATH, SHARD), tiles, tiles, P(), P(), P()),
        out_specs=(P(PATH, SHARD), tiles, tiles),
        check_vma=False,
    )
```

```python
import jax
import jax.numpy as jnp
from jax import lax
from jax.experimental import pallas as pl
from jax.experimental.pallas import tpu as pltpu
from jax.sharding import Mesh, PartitionSpec as P

MODULES = 4
BLK = 128
MU = 0.9
LR_INNER = 0.05
LR_OUTER = 0.02

PATH = ("yh", "x")
SHARD = ("yl", "z", "c")
BIG = ("x", "yh")
VMEM_LIMIT = 24 * 1024 * 1024


def pack_kernel(here_ref, cluster_hbm, tokens_hbm, cotangent_hbm, send_hbm, cluster_ref, tokens_ref, cotangent_ref, in_sem, out_sem):
    blocks = tokens_ref.shape[1] // BLK
    pairs = ((cluster_hbm, cluster_ref), (tokens_hbm, tokens_ref), (cotangent_hbm, cotangent_ref))
    loads = [pltpu.make_async_copy(there, here, in_sem.at[i]) for i, (there, here) in enumerate(pairs)]
    for load in loads:
        load.start()
    for load in loads:
        load.wait()
    saves = []
    for b in range(blocks):
        to = cluster_ref[here_ref[0] * blocks + b]
        for i, source in enumerate((tokens_ref, cotangent_ref)):
            lanes = source.at[:, pl.ds(b * BLK, BLK)]
            saves.append(pltpu.make_async_copy(lanes, send_hbm.at[to, i], out_sem.at[2 * b + i]))
            saves[-1].start()
    for save in saves:
        save.wait()


def grads_kernel(
    place_ref, core_ref, w_ref, mine_hbm, other_hbm, delta_hbm, dgu_hbm, xp, yp, delta, dgu, g_s, u_s, d_s, h_s, in_sem, out_sem
):
    owners, _, units, width = w_ref.shape

    def fetch(source, target, base):
        for o in range(owners):
            here = pl.ds(pl.multiple_of(place_ref[o] * width, width), width)
            pltpu.make_async_copy(source.at[here], target.at[pl.ds(o * width, width)], in_sem.at[base + o]).start()

    @pl.when(core_ref[0] == 0)
    def _():
        fetch(mine_hbm, xp, 0)
        fetch(other_hbm, yp, owners)

    @pl.when(core_ref[0] != 0)
    def _():
        fetch(other_hbm, xp, 0)
        fetch(mine_hbm, yp, owners)

    def arrived(target, base, some):
        for o in some:
            rows = pl.ds(o * width, width)
            pltpu.make_async_copy(mine_hbm.at[rows], target.at[rows], in_sem.at[base + o]).wait()

    def product(k, tokens, some):
        left = jnp.concatenate([w_ref[o, k] for o in some], axis=1)
        right = tokens[some[0] * width : (some[-1] + 1) * width, :]
        return jnp.dot(left, right, preferred_element_type=jnp.float32)

    early, late = range(owners // 2), range(owners // 2, owners)
    arrived(xp, 0, early)
    g_s[...] = product(0, xp, early)
    u_s[...] = product(1, xp, early)
    arrived(xp, 0, late)
    g_s[...] += product(0, xp, late)
    u_s[...] += product(1, xp, late)
    arrived(yp, owners, early)
    d_s[...] = product(2, yp, early)
    arrived(yp, owners, late)
    d_s[...] += product(2, yp, late)
    step = 32

    def act(i, carry):
        at = pl.multiple_of(i * step, step)
        rows = pl.ds(at, step)
        gate = g_s[rows, :]
        up = u_s[rows, :]
        dh = d_s[rows, :]
        sig = jax.nn.sigmoid(gate)
        silu = gate * sig
        h_s[rows, :] = (silu * up).astype(jnp.bfloat16)
        dgu[rows, :] = (dh * up * sig * (1.0 + gate * (1.0 - sig))).astype(jnp.bfloat16)
        dgu[pl.ds(pl.multiple_of(units + at, step), step), :] = (dh * silu).astype(jnp.bfloat16)
        return carry

    lax.fori_loop(0, units // step, act, 0)
    save_dgu = pltpu.make_async_copy(dgu, dgu_hbm, out_sem.at[owners // 2])
    save_dgu.start()
    nt = (((1,), (1,)), ((), ()))
    saves = []
    for p in range(owners // 2):
        rows = slice(p * 2 * width, (p + 1) * 2 * width)
        gu = LR_INNER * lax.dot_general(dgu[...], xp[rows, :], nt, preferred_element_type=jnp.float32)
        dn = LR_INNER * lax.dot_general(h_s[...], yp[rows, :], nt, preferred_element_type=jnp.float32)
        gu = gu.astype(jnp.bfloat16)
        dn = dn.astype(jnp.bfloat16)
        for half in range(2):
            lanes = slice(half * width, (half + 1) * width)
            delta[2 * p + half, 0] = gu[:units, lanes]
            delta[2 * p + half, 1] = gu[units:, lanes]
            delta[2 * p + half, 2] = dn[:, lanes]
        pair = slice(2 * p, 2 * p + 2)
        save = pltpu.make_async_copy(delta.at[pair], delta_hbm.at[pair], out_sem.at[p])
        save.start()
        saves.append(save)
    for save in saves:
        save.wait()
    save_dgu.wait()


def input_kernel(slot_ref, core_ref, w_ref, dgu_ref, keep_ref, give_ref):
    owners, _, units, width = w_ref.shape
    half = width // 2
    core = core_ref[0]

    for o in range(owners):
        w = w_ref[o, 0:2].reshape(2 * units, width)
        part = lax.dot_general(w, dgu_ref[...], (((0,), (0,)), ((), ())), preferred_element_type=jnp.float32)
        j = slot_ref[o]
        low, high = part[:half], part[half:]
        keep_ref[j] = jnp.where(core == 0, low, high)
        give_ref[j] = jnp.where(core == 0, high, low).astype(jnp.bfloat16)


def pair_kernel(keep_ref, came_ref, own_ref, *out_refs):
    for k in range(len(out_refs) + 1):
        at = slice(2 * k, 2 * k + 2)
        total = keep_ref[at] + came_ref[at].astype(jnp.float32)
        if k == 0:
            own_ref[...] = total
        else:
            out_refs[k - 1][...] = total.astype(jnp.bfloat16)


def update_kernel(
    module_ref,
    scale_ref,
    delta_hbm,
    w_ref,
    m_ref,
    ours_ref,
    theirs_ref,
    new_w_hbm,
    new_m_hbm,
    grad_ref,
    delta_ref,
    new_w,
    new_m,
    acc,
    in_sem,
    out_sem,
):
    modules, mats, units, width = w_ref.shape
    paths = delta_ref.shape[0]
    step = acc.shape[1]
    parts = [(k, slice(i * step, (i + 1) * step)) for k in range(mats) for i in range(units // step)]
    loads = []
    for k, rows in parts:
        part = (slice(None), k, rows)
        loads.append(pltpu.make_async_copy(delta_hbm.at[part], delta_ref.at[part], in_sem.at[len(loads)]))
        loads[-1].start()
    grad_ref[...] = (ours_ref[...] + theirs_ref[...]).astype(grad_ref.dtype)
    saves = []
    for load, (k, rows) in zip(loads, parts):
        load.wait()
        acc[...] = jnp.zeros_like(acc)
        for q in range(paths):
            acc[module_ref[q]] += delta_ref[q, k, rows, :].astype(jnp.float32)
        for m in range(modules):
            mean = acc[m] * scale_ref[m]
            moment = MU * m_ref[m, k, rows, :] + mean
            new_m[m, k, rows, :] = moment
            new_w[m, k, rows, :] = w_ref[m, k, rows, :].astype(jnp.float32) - LR_OUTER * (mean + MU * moment)
        for here, there in ((new_w, new_w_hbm), (new_m, new_m_hbm)):
            part = (slice(None), k, rows)
            save = pltpu.make_async_copy(here.at[part], there.at[part], out_sem.at[len(saves)])
            save.start()
            saves.append(save)
    for save in saves:
        save.wait()


def in_hbm(array):
    return pltpu.with_memory_space_constraint(array, pltpu.HBM)


def pack(here, cluster, tokens, cotangent):
    cols, rows = tokens.shape
    blocks = rows // BLK
    paths = cluster.shape[0] // blocks
    smem = pl.BlockSpec(memory_space=pltpu.SMEM)
    hbm = pl.BlockSpec(memory_space=pltpu.HBM)
    return pl.pallas_call(
        pack_kernel,
        out_shape=pltpu.HBM((paths, 2, cols, BLK), tokens.dtype),
        in_specs=[smem, hbm, hbm, hbm],
        out_specs=hbm,
        scratch_shapes=[
            pltpu.SMEM(cluster.shape, cluster.dtype),
            pltpu.VMEM(tokens.shape, tokens.dtype),
            pltpu.VMEM(tokens.shape, tokens.dtype),
            pltpu.SemaphoreType.DMA((3,)),
            pltpu.SemaphoreType.DMA((2 * blocks,)),
        ],
        compiler_params=pltpu.CompilerParams(vmem_limit_bytes=VMEM_LIMIT),
        cost_estimate=pl.CostEstimate(flops=1000, bytes_accessed=1000, transcendentals=0),
        name="pack",
    )(here, in_hbm(cluster), in_hbm(tokens), in_hbm(cotangent))


def grads(place, core, w, mine, other):
    owners, _, units, width = w.shape
    rows = mine.shape[1]
    smem = pl.BlockSpec(memory_space=pltpu.SMEM)
    vmem = pl.BlockSpec(memory_space=pltpu.VMEM)
    hbm = pl.BlockSpec(memory_space=pltpu.HBM)
    return pl.pallas_call(
        grads_kernel,
        out_shape=(
            pltpu.HBM(w.shape, jnp.bfloat16),
            pltpu.HBM((2 * units, rows), jnp.bfloat16),
        ),
        in_specs=[smem, smem, vmem, hbm, hbm],
        out_specs=(hbm, hbm),
        scratch_shapes=[
            pltpu.VMEM(mine.shape, jnp.bfloat16),
            pltpu.VMEM(mine.shape, jnp.bfloat16),
            pltpu.VMEM(w.shape, jnp.bfloat16),
            pltpu.VMEM((2 * units, rows), jnp.bfloat16),
            pltpu.VMEM((units, rows), jnp.float32),
            pltpu.VMEM((units, rows), jnp.float32),
            pltpu.VMEM((units, rows), jnp.float32),
            pltpu.VMEM((units, rows), jnp.bfloat16),
            pltpu.SemaphoreType.DMA((2 * owners,)),
            pltpu.SemaphoreType.DMA((owners // 2 + 1,)),
        ],
        compiler_params=pltpu.CompilerParams(vmem_limit_bytes=VMEM_LIMIT),
        cost_estimate=pl.CostEstimate(
            flops=12 * units * rows * owners * width, bytes_accessed=12 * 2**20, transcendentals=units * rows
        ),
        name="grads",
    )(place, core, w, in_hbm(mine), in_hbm(other))


def input_partial(slot_of, core, w, dgu):
    owners, _, units, width = w.shape
    rows = dgu.shape[1]
    smem = pl.BlockSpec(memory_space=pltpu.SMEM)
    vmem = pl.BlockSpec(memory_space=pltpu.VMEM)
    shape = (owners, width // 2, rows)
    return pl.pallas_call(
        input_kernel,
        out_shape=(jax.ShapeDtypeStruct(shape, jnp.float32), jax.ShapeDtypeStruct(shape, jnp.bfloat16)),
        in_specs=[smem, smem, vmem, vmem],
        out_specs=(vmem, vmem),
        compiler_params=pltpu.CompilerParams(vmem_limit_bytes=VMEM_LIMIT),
        cost_estimate=pl.CostEstimate(flops=1000, bytes_accessed=1000, transcendentals=0),
        name="input_partial",
    )(slot_of, core, w, dgu)


def pair_sums(keep, came):
    tiles, feats, rows = keep.shape
    vmem = pl.BlockSpec(memory_space=pltpu.VMEM)
    part = (2, feats, rows)
    steps = tiles // 2
    return pl.pallas_call(
        pair_kernel,
        out_shape=(jax.ShapeDtypeStruct(part, jnp.float32),)
        + (jax.ShapeDtypeStruct(part, jnp.bfloat16),) * (steps - 1),
        in_specs=[vmem, vmem],
        out_specs=(vmem,) * steps,
        compiler_params=pltpu.CompilerParams(vmem_limit_bytes=VMEM_LIMIT),
        cost_estimate=pl.CostEstimate(flops=1000, bytes_accessed=1000, transcendentals=0),
        name="pair_sums",
    )(keep, came)


def update(modules_of, scale, delta, owned, momentum, ours, theirs):
    modules, mats, units, width = owned.shape
    smem = pl.BlockSpec(memory_space=pltpu.SMEM)
    vmem = pl.BlockSpec(memory_space=pltpu.VMEM)
    hbm = pl.BlockSpec(memory_space=pltpu.HBM)
    return pl.pallas_call(
        update_kernel,
        out_shape=(jax.ShapeDtypeStruct(momentum.shape, jnp.float32),) * 2
        + (jax.ShapeDtypeStruct(ours.shape, jnp.bfloat16),),
        in_specs=[smem, smem, hbm, vmem, vmem, vmem, vmem],
        out_specs=(hbm, hbm, vmem),
        scratch_shapes=[
            pltpu.VMEM(delta.shape, delta.dtype),
            pltpu.VMEM(momentum.shape, jnp.float32),
            pltpu.VMEM(momentum.shape, jnp.float32),
            pltpu.VMEM((modules, units // 2, width), jnp.float32),
            pltpu.SemaphoreType.DMA((2 * mats,)),
            pltpu.SemaphoreType.DMA((4 * mats,)),
        ],
        compiler_params=pltpu.CompilerParams(vmem_limit_bytes=VMEM_LIMIT // 2),
        cost_estimate=pl.CostEstimate(flops=10**6, bytes_accessed=8 * 2**20, transcendentals=0),
        name="update",
    )(modules_of, scale, in_hbm(delta), owned, momentum, ours, theirs)


def pick(array, index):
    return array.at[index].get(mode="promise_in_bounds")


def transposed(per_path):
    lead = per_path.shape[:-1]
    grid = per_path.reshape(lead + tuple(lax.axis_size(name) for name in PATH))
    return jnp.swapaxes(grid, -1, -2).reshape(per_path.shape)


def turn(size, k):
    return [(i, (i + k) % size) for i in range(size)]


def ring_gather(piece, beside):
    depth = lax.axis_size("z")
    first = lax.axis_index("yl") == 0
    pair = jnp.concatenate([jnp.where(first, piece, beside), jnp.where(first, beside, piece)], axis=0)
    half = piece.shape[0]
    up = down = pair
    parts = [pair]
    at = [0] * depth
    for k in range(1, depth // 2):
        up = lax.ppermute(up, "z", turn(depth, 1))
        down = lax.ppermute(down, "z", turn(depth, -1))
        at[depth - k] = len(parts)
        at[k] = len(parts) + 1
        parts += [up, down]
    at[depth // 2] = len(parts)
    parts.append(lax.ppermute(up[:half], "z", turn(depth, 1)))
    parts.append(lax.ppermute(down[half:], "z", turn(depth, -1)))
    return jnp.concatenate(parts, axis=0), at


def body(tokens, cotangent, weights, momentum, cluster, path_module, owner):
    paths = lax.axis_size(PATH)
    here = lax.axis_index(PATH)
    core = lax.axis_index("c")
    modules_of = path_module[:, 0]
    path_ids = jnp.arange(paths, dtype=jnp.int32)
    blocks = tokens.shape[0] // BLK
    cols = tokens.shape[1]
    owned = weights[0]

    block_ids = jnp.arange(blocks, dtype=jnp.int32)
    send_x = pack(here.reshape(1), cluster, tokens.T, cotangent.T)
    recv_x = lax.all_to_all(
        send_x.reshape(paths * 2, cols, BLK), PATH + ("c",), split_axis=0, concat_axis=0, tiled=True
    ).reshape(paths, 2, cols, BLK)
    has = jnp.any(cluster.reshape(paths, blocks) == here, axis=1)
    before = jnp.sum((has[None, :] & (path_ids[None, :] < path_ids[:, None])).astype(jnp.int32), axis=1)
    comes = has[None, :] & (before[None, :] == block_ids[:, None])
    sources = jnp.sum(jnp.where(comes, path_ids[None, :], 0), axis=1)
    piece = pick(recv_x, sources).transpose(1, 2, 0, 3).reshape(2 * cols, blocks * BLK)

    beside = lax.ppermute(piece, "yl", [(0, 1), (1, 0)])
    send_w, piece, beside = lax.optimization_barrier((pick(owned, transposed(modules_of)), piece, beside))
    recv_w = lax.all_to_all(send_w, BIG, split_axis=0, concat_axis=0, tiled=True)
    mine, at = ring_gather(piece, beside)
    swap = [(0, 1), (1, 0)]
    other = lax.ppermute(mine, "c", swap)

    owner_row = owner[modules_of[here]]
    tile_of = jnp.sum(jnp.where(owner_row[None, :] == transposed(path_ids)[:, None], path_ids[None, :], 0), axis=1)
    z = lax.axis_index("z")
    depth = lax.axis_size("z")
    away = (tile_of % depth - z) % depth
    side = tile_of // depth
    place = jnp.sum(jnp.where(away[:, None] == jnp.arange(depth)[None, :], jnp.array(at, jnp.int32)[None, :], 0), axis=1)
    core_id = core.reshape(1)
    delta, dgu = grads(place * 2 + side, core_id, recv_w, mine, other)
    recv_delta = lax.all_to_all(delta, BIG, split_axis=0, concat_axis=0, tiled=True)

    keep, give = input_partial(away * 2 + side, core_id, recv_w, dgu)
    sums = pair_sums(keep, lax.ppermute(give, "c", swap))
    came = [lax.ppermute(sums[k], "z", turn(depth, k)) for k in range(1, depth)]
    total = sums[0]
    for part in came:
        total = total + part.astype(jnp.float32)
    yl = lax.axis_index("yl")
    theirs = lax.ppermute(lax.dynamic_index_in_dim(total, 1 - yl, 0, keepdims=False), "yl", swap)
    member = modules_of[None, :] == jnp.arange(MODULES, dtype=jnp.int32)[:, None]
    counts = jnp.sum(member.astype(jnp.float32), axis=1)
    ours = lax.dynamic_index_in_dim(total, yl, 0, keepdims=False)
    new_tiles, new_moment, grad = update(
        transposed(modules_of), 1.0 / counts, recv_delta, owned, momentum[0], ours, theirs
    )
    input_grad = grad.T
    return (input_grad, new_tiles[None], new_moment[None])


def solution(mesh):
    fine = Mesh(mesh.devices.reshape(4, 4, 2, 8, 2), PATH + SHARD)
    tiles = P(PATH, None, None, SHARD, None)
    return jax.shard_map(
        body,
        mesh=fine,
        in_specs=(P(PATH, SHARD), P(PATH, SHARD), tiles, tiles, P(), P(), P()),
        out_specs=(P(PATH, SHARD), tiles, tiles),
        check_vma=False,
    )
```
